32 devices in a mesh: fsdp: 8 (over y, x, core), tp: 4 (over z).
Axes of the slice: x: 2, y: 2, z: 4, core: 2. Of those that a mesh axis runs over, the one named last changes fastest.
Arguments:
- x_in: bfloat16 [4096, 1600], P(('fsdp', 'tp')), may hold values from -6 to 6
- lengths: int32 [2], replicated, may hold values from 256 to 3840, as said below
- w_q: bfloat16 [2, 1600, 1600], P(None, 'fsdp'), may hold values from -0.15625 to 0.15625
- w_kv: bfloat16 [2, 1600, 640], P(None, 'fsdp'), may hold values from -0.15625 to 0.15625
- w_o: bfloat16 [2, 1600, 1600], P(None, 'fsdp'), may hold values from -0.15625 to 0.15625
- input_weight: bfloat16 [2, 1600, 3, 3200], P(None, 'fsdp', None, 'tp'), may hold values from -0.15625 to 0.15625
- a_log: float32 [2, 3200], P(None, 'tp'), may hold values from -7 to -2
- dt_bias: float32 [2, 3200], P(None, 'tp'), may hold values from -3 to 0
- d_skip: float32 [2, 3200], P(None, 'tp'), may hold values from 0.5 to 1.5
- w_bc: bfloat16 [2, 1600, 32], replicated, may hold values from -0.15625 to 0.15625
- w_out: bfloat16 [2, 3200, 1600], P(None, 'tp', 'fsdp'), may hold values from -0.109375 to 0.109375
- gains: float32 [2, 4, 1600], replicated, may hold values from 0.5 to 1.5
- gate_up_weight: bfloat16 [2, 1600, 2, 5504], P(None, 'fsdp', None, 'tp'), may hold values from -0.15625 to 0.15625
- w_down: bfloat16 [2, 5504, 1600], P(None, 'tp', 'fsdp'), may hold values from -0.078125 to 0.078125
- cotangent: bfloat16 [4096, 1600], P(('fsdp', 'tp')), may hold values from -6 to 6
Outputs:
- block_out: bfloat16 [4096, 1600], P(('fsdp', 'tp'))
- grad_input: float32 [4096, 1600], P(('fsdp', 'tp'))
- grad_w_q: float32 [2, 1600, 1600], P(None, 'fsdp')
- grad_w_kv: float32 [2, 1600, 640], P(None, 'fsdp')
- grad_w_o: float32 [2, 1600, 1600], P(None, 'fsdp')
- grad_w_in: float32 [2, 1600, 3, 3200], P(None, 'fsdp', None, 'tp')
- grad_a_log: float32 [2, 3200], P(None, 'fsdp')
- grad_dt_bias: float32 [2, 3200], P(None, 'fsdp')
- grad_d_skip: float32 [2, 3200], P(None, 'fsdp')
- grad_w_bc: float32 [2, 1600, 32], P(None, 'fsdp')
- grad_w_out: float32 [2, 3200, 1600], P(None, 'tp', 'fsdp')
- grad_gains: float32 [2, 4, 1600], P(None, None, 'fsdp')
- grad_w_gu: float32 [2, 1600, 2, 5504], P(None, 'fsdp', None, 'tp')
- grad_w_down: float32 [2, 5504, 1600], P(None, 'tp', 'fsdp')
The draws below stay inside these ranges and needn't reach their ends.
Inputs may be any that keep to these rules, and one draw needn't show every extreme that they name: The 2 lengths sum to 4096; both 256 and 3840 occur in every draw.
All inputs are finite; a program needn't handle non-finite values.
Results may differ from the reference program's by a relative error of at most 0.033.
Values may be sent and summed in bfloat16 or wider, within the bound.
No kernel may reach another device: no remote copies, remote signals or barrier semaphores. Data moves between devices by JAX's collectives and lax.ppermute only.
A program may use at most 512 MiB of HBM per device.

```python
import math
import jax
import jax.numpy as jnp
from jax import lax

D = 1600
HEADS = 25
HEAD = 64
KV_HEADS = 5
INNER = 3200
STATE = 16
FF = 5504
WINDOW = 1024
LAYERS = 2
SEQLEN = 2048
SHORTEST = 256
TOKENS = 4096
SEQS = 2


def draw_lengths(key, part):
    key = jax.random.fold_in(key, 7)
    pair_count = SEQS // 2
    spread = SEQLEN - SHORTEST
    amount_key, pick_key, order_key = jax.random.split(key, 3)
    amounts = jax.random.randint(amount_key, (pair_count,), 0, spread + 1)
    chosen = jax.random.randint(pick_key, (), 0, pair_count)
    amounts = jnp.where(jnp.arange(pair_count) == chosen, spread, amounts)
    paired = jnp.concatenate([SEQLEN + amounts, SEQLEN - amounts])
    arrangement = jax.random.permutation(order_key, SEQS)
    return paired[arrangement].astype(jnp.int32)


def levels(key, dims, cuts, low, top_value):
    def one(position, parts):
        steps = jax.random.uniform(jax.random.fold_in(jax.random.fold_in(key, 6), position), (parts,), jnp.float32, low / len(cuts), top_value / len(cuts))
        return jnp.repeat(jnp.exp(steps), dims[position] // parts).reshape((-1,) + (1,) * (len(dims) - position - 1))

    loudness = one(*cuts[0])
    for cut in cuts[1:]:
        loudness = loudness * one(*cut)
    return loudness


def scatter_about(key, shape, deviation, most, cuts=(), kind=jnp.bfloat16):
    loudness = levels(key, shape, cuts, -0.22, 0.18) if cuts else 1.0
    values = jax.random.normal(key, shape, jnp.float32) * deviation * loudness
    return jnp.minimum(jnp.maximum(values, -most), most).astype(kind)


def setup_inputs(seed: int = 0) -> dict:
    splits = jax.random.split(jax.random.key(seed), 16)
    return {
        "x_in": scatter_about(splits[0], (TOKENS, D), 1.0, 6.0, ((0, 32),)),
        "lengths": draw_lengths(jax.random.fold_in(splits[15], 71), 0),
        "w_q": scatter_about(splits[2], (LAYERS, D, HEADS * HEAD), D ** -0.5, 0.15625, ((1, 8),)),
        "w_kv": scatter_about(splits[3], (LAYERS, D, 2 * KV_HEADS * HEAD), D ** -0.5, 0.15625, ((1, 8),)),
        "w_o": scatter_about(splits[4], (LAYERS, HEADS * HEAD, D), (HEADS * HEAD) ** -0.5, 0.15625, ((1, 8),)),
        "input_weight": scatter_about(splits[5], (LAYERS, D, 3, INNER), D ** -0.5, 0.15625, ((1, 8), (3, 4))),
        "a_log": jnp.clip(-7.0 + 5.0 * jax.random.uniform(splits[6], (LAYERS, INNER), jnp.float32) ** levels(splits[6], (LAYERS, INNER), ((1, 4),), -0.2, 0.2), -7.0, -2.0),
        "dt_bias": jnp.clip(-3.0 + 3.0 * jax.random.uniform(splits[7], (LAYERS, INNER), jnp.float32) ** levels(splits[7], (LAYERS, INNER), ((1, 4),), -0.2, 0.2), -3.0, 0.0),
        "d_skip": jnp.clip(0.5 + 1.0 * jax.random.uniform(splits[8], (LAYERS, INNER), jnp.float32) ** levels(splits[8], (LAYERS, INNER), ((1, 4),), -0.2, 0.2), 0.5, 1.5),
        "w_bc": scatter_about(splits[9], (LAYERS, D, 2 * STATE), D ** -0.5, 0.15625),
        "w_out": scatter_about(splits[10], (LAYERS, INNER, D), INNER ** -0.5, 0.109375, ((1, 4), (2, 8))),
        "gains": jnp.clip(1.0 + 0.1 * jax.random.normal(splits[11], (LAYERS, 4, D), jnp.float32), 0.5, 1.5),
        "gate_up_weight": scatter_about(splits[12], (LAYERS, D, 2, FF), D ** -0.5, 0.15625, ((1, 8), (3, 4))),
        "w_down": scatter_about(splits[13], (LAYERS, FF, D), FF ** -0.5, 0.078125, ((1, 4), (2, 8))),
        "cotangent": scatter_about(splits[14], (TOKENS, D), 1.0, 6.0, ((0, 32),)),
    }


@jax.custom_vjp
def low(v):
    return lax.optimization_barrier(v.astype(jnp.bfloat16)).astype(jnp.float32)

@jax.custom_vjp
def reduced_backward_pass(v):
    return v

def low_keep(v):
    return (low(v), None)

def low_pass(kept, grad):
    return (grad,)

def back_keep(v):
    return (v, None)

def back_low(kept, grad):
    return (low(grad),)
low.defvjp(low_keep, low_pass)
reduced_backward_pass.defvjp(back_keep, back_low)
EPSILON = 1e-05
TOP_PRECISION = lax.Precision.HIGHEST

def matmul(left_side, right_side):
    return jnp.dot(left_side, right_side, precision=TOP_PRECISION, preferred_element_type=jnp.float32)

def rounded(values):
    return reduced_backward_pass(low(values))

def rms_scale(values, gain_row):
    return values * lax.rsqrt(lax.optimization_barrier(jnp.mean(values * values, axis=-1, keepdims=True)) + EPSILON) * gain_row

def sequence_ids(lengths, places):
    seq_ends = jnp.cumsum(lengths).astype(jnp.int32)
    starts = (seq_ends - lengths).astype(jnp.int32)
    numbers = lax.optimization_barrier(jnp.sum((places[:, None] >= starts[None, :]).astype(jnp.int32), axis=1)).astype(jnp.int32) - 1
    opening = jnp.any(places[:, None] == starts[None, :], axis=1)
    return (numbers, opening)

def window_attention(queries, keys_all, values_all, numbers):
    row_count = queries.shape[0]
    block_rows = math.gcd(row_count, 512)
    group_size = HEADS // KV_HEADS
    keys_pad = jnp.pad(keys_all, ((WINDOW, 0), (0, 0), (0, 0)))
    values_pad = jnp.pad(values_all, ((WINDOW, 0), (0, 0), (0, 0)))
    numbers_pad = jnp.concatenate([jnp.full((WINDOW,), -1, jnp.int32), numbers.astype(jnp.int32)])
    offsets = (jnp.arange(block_rows)[:, None] + WINDOW - jnp.arange(block_rows + WINDOW)[None, :]).astype(jnp.int32)

    def one_block(block_index):
        row_start = (block_index * block_rows).astype(jnp.int32)
        query_rows = lax.dynamic_slice_in_dim(queries, row_start, block_rows, 0).reshape(block_rows, KV_HEADS, group_size, HEAD)
        key_rows = lax.dynamic_slice_in_dim(keys_pad, row_start, block_rows + WINDOW, 0)
        value_rows = lax.dynamic_slice_in_dim(values_pad, row_start, block_rows + WINDOW, 0)
        key_numbers = lax.dynamic_slice_in_dim(numbers_pad, row_start, block_rows + WINDOW, 0)
        query_numbers = lax.dynamic_slice_in_dim(numbers, row_start, block_rows, 0)
        scores = reduced_backward_pass(jnp.einsum('tkgd,skd->kgts', query_rows, key_rows, precision=TOP_PRECISION) * 0.125)
        allowed = (offsets >= 0) & (offsets < WINDOW) & (query_numbers[:, None] == key_numbers[None, :])
        scores = jnp.where(allowed, scores, -1e+30)
        weights = jax.nn.softmax(scores, axis=-1)
        mixture = jnp.einsum('kgts,skd->tkgd', low(weights), value_rows, precision=TOP_PRECISION)
        return mixture.reshape(block_rows, HEADS * HEAD)
    outputs = lax.map(jax.checkpoint(one_block), jnp.arange(row_count // block_rows, dtype=jnp.int32))
    return outputs.reshape(row_count, HEADS * HEAD)

def selective_scan(inflow_u, step_sizes, b_rows, c_rows, rate, opening):
    row_count = inflow_u.shape[0]
    block_rows = math.gcd(row_count, 256)

    def token_step(carry_state, row_slices):
        u_row, step_row, b_row, c_row, open_row = row_slices
        survive = jnp.exp(step_row * rate) * (1.0 - open_row)
        carry_state = survive[:, None] * carry_state + (step_row * u_row)[:, None] * b_row[None, :]
        return (carry_state, lax.optimization_barrier(jnp.sum(carry_state * c_row[None, :], axis=1)))

    def block_step(carry_state, row_slices):
        return lax.scan(token_step, carry_state, row_slices)
    shaped = tuple((part.reshape((row_count // block_rows, block_rows) + part.shape[1:]) for part in (inflow_u, step_sizes, b_rows, c_rows, opening)))
    start_state = jnp.zeros((INNER, STATE), jnp.float32)
    _, outputs = lax.scan(jax.checkpoint(block_step), start_state, shaped)
    return outputs.reshape(row_count, INNER)

def hymba_layer(stream, numbers, opening, w_q, w_kv, w_o, input_weight, a_log, dt_bias, d_skip, w_bc, w_out, gains, gate_up_weight, w_down):
    normalized_rows = low(rms_scale(stream, gains[0]))
    queries = rounded(matmul(normalized_rows, w_q)).reshape(-1, HEADS, HEAD)
    key_value = rounded(matmul(normalized_rows, w_kv))
    kv_width = KV_HEADS * HEAD
    keys_all = key_value[:, :kv_width].reshape(-1, KV_HEADS, HEAD)
    values_all = key_value[:, kv_width:].reshape(-1, KV_HEADS, HEAD)
    attended = rounded(window_attention(queries, keys_all, values_all, numbers))
    attn_out = reduced_backward_pass(matmul(attended, w_o))
    projected_rows = reduced_backward_pass(jnp.einsum('pu,usw->psw', normalized_rows, input_weight, precision=TOP_PRECISION))
    inflow_u = projected_rows[:, 0]
    gate_z = projected_rows[:, 1]
    step_sizes = jax.nn.softplus(projected_rows[:, 2] + dt_bias)
    bc_rows = matmul(normalized_rows, w_bc)
    scanned = selective_scan(inflow_u, step_sizes, bc_rows[:, :STATE], bc_rows[:, STATE:], -jnp.exp(a_log), opening)
    mamba_mid = low((scanned + d_skip * inflow_u) * jax.nn.silu(gate_z))
    mamba_out = reduced_backward_pass(matmul(mamba_mid, w_out))
    mixture = 0.5 * (rms_scale(attn_out, gains[1]) + rms_scale(mamba_out, gains[2]))
    middle = stream + mixture
    feedforward_input = low(rms_scale(middle, gains[3]))
    gate_up_product = reduced_backward_pass(jnp.einsum('pu,usw->psw', feedforward_input, gate_up_weight, precision=TOP_PRECISION))
    hidden = low(jax.nn.silu(gate_up_product[:, 0]) * gate_up_product[:, 1])
    return middle + reduced_backward_pass(matmul(hidden, w_down))

def reference(x_in, lengths, w_q, w_kv, w_o, input_weight, a_log, dt_bias, d_skip, w_bc, w_out, gains, gate_up_weight, w_down, cotangent):
    numbers, opening = sequence_ids(lengths, jnp.arange(TOKENS, dtype=jnp.int32))
    opening = opening.astype(jnp.float32)
    floats = tuple((item.astype(jnp.float32) for item in (x_in, w_q, w_kv, w_o, input_weight, a_log, dt_bias, d_skip, w_bc, w_out, gains, gate_up_weight, w_down)))

    def forward(stream, w_q, w_kv, w_o, input_weight, a_log, dt_bias, d_skip, w_bc, w_out, gains, gate_up_weight, w_down):
        for layer_index in range(LAYERS):
            stream = hymba_layer(stream, numbers, opening, w_q[layer_index], w_kv[layer_index], w_o[layer_index], input_weight[layer_index], a_log[layer_index], dt_bias[layer_index], d_skip[layer_index], w_bc[layer_index], w_out[layer_index], gains[layer_index], gate_up_weight[layer_index], w_down[layer_index])
        return stream
    result, pullback = jax.vjp(forward, *floats)
    gradients = pullback(cotangent.astype(jnp.float32))
    return (result.astype(jnp.bfloat16), gradients[0], gradients[1], gradients[2], gradients[3], gradients[4], gradients[5], gradients[6], gradients[7], gradients[8], gradients[9], gradients[10], gradients[11], gradients[12])
```

```python
import functools

import jax
import jax.numpy as jnp
from jax import lax
from jax.experimental import pallas as pl
from jax.experimental.pallas import tpu as pltpu
from jax.sharding import Mesh
from jax.sharding import PartitionSpec as P

HEADS = 25
HEAD = 64
KV_HEADS = 5
GROUP = HEADS // KV_HEADS
WINDOW = 1024
STATE = 16
EPSILON = 1e-05
TOP_PRECISION = lax.Precision.HIGHEST

CORES = 2
CHUNKS = 8
AT_ONCE = 4
LANES = 128
SLOTS = 2
VMEM_BYTES = 56 * 1024 * 1024
F32 = jnp.float32
BF16 = jnp.bfloat16


def round_up(value, unit):
    return -(-value // unit) * unit


def dot(a, b, out=F32):
    return jnp.dot(a, b, preferred_element_type=F32).astype(out)


def dot_nt(a, b, out=F32):
    return lax.dot_general(
        a, b, (((1,), (1,)), ((), ())), preferred_element_type=F32
    ).astype(out)


def dot_tn(a, b, out=F32):
    return lax.dot_general(
        a, b, (((0,), (0,)), ((), ())), preferred_element_type=F32
    ).astype(out)


def rms_scale(values, gain_row):
    return (
        values * lax.rsqrt(jnp.mean(values * values, axis=-1, keepdims=True) + EPSILON) * gain_row
    )


def branch_mix(attn_out, mamba_out, gain_attn, gain_mamba):
    return 0.5 * (rms_scale(attn_out, gain_attn) + rms_scale(mamba_out, gain_mamba))


def swiglu(gate_up_product):
    half = gate_up_product.shape[1] // 2
    return jax.nn.silu(gate_up_product[:, :half]) * gate_up_product[:, half:]


def softplus(v):
    return jnp.maximum(v, 0.0) + jnp.log1p(jnp.exp(-jnp.abs(v)))


def sigmoid(v):
    return 1.0 / (1.0 + jnp.exp(-v))


def kernel_params(bytes_limit=VMEM_BYTES):
    return pltpu.CompilerParams(
        dimension_semantics=("arbitrary",), vmem_limit_bytes=bytes_limit
    )


def cost(flops, moved):
    return pl.CostEstimate(flops=int(flops), bytes_accessed=int(moved), transcendentals=0)


def spread_bc(bc_ref, spread, turned, length):
    def turn(s, carry):
        place = pl.ds(pl.multiple_of(s * CHUNKS, CHUNKS), CHUNKS)
        turned[place, :] = bc_ref[pl.ds(s, CHUNKS, stride=length), :]
        return carry

    lax.fori_loop(0, length, turn, 0, unroll=8)
    block = 2 * LANES
    for q in range(2 * STATE * LANES // block):
        row = lax.broadcasted_iota(jnp.int32, (LANES, block), 0)
        column = lax.broadcasted_iota(jnp.int32, (LANES, block), 1) + q * block
        pick = (row == column // LANES).astype(F32).astype(BF16)
        for r in range(CHUNKS * length // block):
            part = slice(r * block, (r + 1) * block)
            spread[part, q * block : (q + 1) * block] = jnp.dot(
                turned[part, :].astype(BF16), pick, preferred_element_type=F32
            )


def spread_at(spread, s, n):
    place = pl.ds(pl.multiple_of(s * CHUNKS, CHUNKS), CHUNKS)
    return spread[place, n * LANES : (n + 1) * LANES]


def wide_lanes(t):
    return slice(t * LANES, (t + 1) * LANES)


def put(ref, value):
    for t in range(ref.shape[0]):
        ref[t] = value[:, wide_lanes(t)]


def get(ref, rows):
    return jnp.concatenate([ref[t, rows, :] for t in range(ref.shape[0])], axis=1)


def put_rows(ref, rows, value):
    for t in range(ref.shape[0]):
        ref[t, rows, :] = value[:, wide_lanes(t)]


def fill_decay(u_ref, pre_ref, keep_ref, par_ref, decay, inflow, count):
    step = softplus(pre_ref[...] + par_ref[1:2, :])
    keep = jnp.concatenate([keep_ref[...]] * count, axis=1)
    put(decay, jnp.exp(-step * jnp.exp(par_ref[0:1, :])) * keep)
    if u_ref is not None:
        put(inflow, step * u_ref[...])


def state_at(n):
    return slice(n * CHUNKS, (n + 1) * CHUNKS)


def stepped(refs, rows):
    return [[[ref[t, part, :] for t in range(ref.shape[0])] for part in rows] for ref in refs]


def before_kernel(length, count, me_ref, u_ref, pre_ref, bc_ref, keep_ref, par_ref, ends_ref, tail_ref, dev_ref, decay, inflow, ends):
    fill_decay(u_ref, pre_ref, keep_ref, par_ref, decay, inflow, count)

    def walk(k, rest):
        rows = pl.ds(length - 1 - k, CHUNKS, stride=length)
        for t in range(count):
            inflow[t, rows, :] = inflow[t, rows, :] * rest[t]
        return tuple(rest[t] * decay[t, rows, :] for t in range(count))

    ones = jnp.ones((CHUNKS, LANES), F32)
    rest = lax.fori_loop(0, length, walk, (ones,) * count, unroll=8)
    tail_ref[...] = jnp.concatenate(rest, axis=1)
    for r in range(CHUNKS):
        part = pl.ds(r * length, length)
        end = lax.dot_general(
            bc_ref[part, :].astype(BF16),
            get(inflow, part).astype(BF16),
            (((0,), (0,)), ((), ())),
            preferred_element_type=F32,
        )
        put_rows(ends, pl.ds(r, STATE, stride=CHUNKS), end[:STATE])
    ends_ref[...] = get(ends, slice(None))
    state = jnp.zeros((STATE, count * LANES), F32)
    total = jnp.ones((1, count * LANES), F32)
    for j in range(CHUNKS):
        r = me_ref[0] ^ j
        fade = tail_ref[pl.ds(r, 1), :]
        state = fade * state + get(ends, pl.ds(r, STATE, stride=CHUNKS))
        total = total * fade
    dev_ref[0:STATE, :] = state
    dev_ref[STATE : STATE + 8, :] = jnp.broadcast_to(total, (8, count * LANES))


def scan_kernel(
    length, count, me_ref, u_ref, gate_ref, pre_ref, bc_ref, keep_ref, par_ref, ends_ref, tail_ref, carried_ref,
    mid_ref, scanned_ref, start_ref, spread, turned, decay, inflow, scanned, ends, start,
):
    @pl.when(pl.program_id(0) == 0)
    def _():
        spread_bc(bc_ref, spread, turned, length)

    fill_decay(u_ref, pre_ref, keep_ref, par_ref, decay, inflow, count)
    put(ends, ends_ref[...])
    state = carried_ref[...]
    for j in range(CHUNKS):
        r = me_ref[0] ^ j
        rows = pl.ds(r, STATE, stride=CHUNKS)
        put_rows(start, rows, state)
        state = tail_ref[pl.ds(r, 1), :] * state + get(ends, rows)
    start_ref[...] = get(start, slice(None))

    def walk(i, carry):
        steps = [i * AT_ONCE + k for k in range(AT_ONCE)]
        rows = [pl.ds(s, CHUNKS, stride=length) for s in steps]
        a, x = stepped((decay, inflow), rows)
        sums = [[None] * count for _ in steps]
        for n in range(STATE):
            b = [spread_at(spread, s, n) for s in steps]
            c = [spread_at(spread, s, STATE + n) for s in steps]
            for t in range(count):
                h = start[t, state_at(n), :]
                for k in range(AT_ONCE):
                    h = a[k][t] * h + x[k][t] * b[k]
                    term = h * c[k]
                    sums[k][t] = term if n == 0 else sums[k][t] + term
                start[t, state_at(n), :] = h
        for k, part in enumerate(rows):
            for t in range(count):
                scanned[t, part, :] = sums[k][t]
        return carry

    lax.fori_loop(0, length // AT_ONCE, walk, 0)
    gate = gate_ref[...]
    y = get(scanned, slice(None))
    scanned_ref[...] = y
    mid_ref[...] = ((y + par_ref[2:3, :] * u_ref[...]) * (gate * sigmoid(gate))).astype(BF16)


def after_kernel(length, count, me_ref, grad_ref, gate_ref, pre_ref, bc_ref, keep_ref, par_ref, tail_ref, heads_ref, dev_ref, decay, flow, heads):
    fill_decay(None, pre_ref, keep_ref, par_ref, decay, None, count)
    gate = gate_ref[...]
    put(flow, grad_ref[...] * (gate * sigmoid(gate)))

    def walk(s, run):
        rows = pl.ds(s, CHUNKS, stride=length)
        new = []
        for t in range(count):
            new.append(run[t] * decay[t, rows, :])
            flow[t, rows, :] = flow[t, rows, :] * new[t]
        return tuple(new)

    lax.fori_loop(0, length, walk, (jnp.ones((CHUNKS, LANES), F32),) * count, unroll=8)
    for r in range(CHUNKS):
        part = pl.ds(r * length, length)
        head = lax.dot_general(
            bc_ref[part, :].astype(BF16),
            get(flow, part).astype(BF16),
            (((0,), (0,)), ((), ())),
            preferred_element_type=F32,
        )
        put_rows(heads, pl.ds(r, STATE, stride=CHUNKS), head[STATE : 2 * STATE])
    heads_ref[...] = get(heads, slice(None))
    state = jnp.zeros((STATE, count * LANES), F32)
    for j in range(CHUNKS - 1, -1, -1):
        r = me_ref[0] ^ j
        state = tail_ref[pl.ds(r, 1), :] * state + get(heads, pl.ds(r, STATE, stride=CHUNKS))
    dev_ref[...] = state


def scan_back_kernel(
    length, count, me_ref, grad_ref, u_ref, gate_ref, pre_ref, bc_ref, keep_ref, par_ref, tail_ref, scanned_ref, start_ref,
    heads_ref, carried_ref, pick_b_ref, pick_c_ref,
    gu_ref, gz_ref, gp_ref, gbc_ref, gpar_ref,
    spread, products, decay, inflow, flow, gx, glog, packed, later, heads, start, mixed, log_sum,
):
    @pl.when(pl.program_id(0) == 0)
    def _():
        spread_bc(bc_ref, spread, mixed, length)
        mixed[...] = jnp.zeros_like(mixed)

    fill_decay(u_ref, pre_ref, keep_ref, par_ref, decay, inflow, count)
    gate = gate_ref[...]
    g = grad_ref[...] * (gate * sigmoid(gate))
    put(flow, g)
    put(gx, g * scanned_ref[...])
    put(heads, heads_ref[...])
    put(start, start_ref[...])
    state = carried_ref[...]
    for j in range(CHUNKS - 1, -1, -1):
        r = me_ref[0] ^ j
        rows = pl.ds(r, STATE, stride=CHUNKS)
        put_rows(later, rows, state)
        state = tail_ref[pl.ds(r, 1), :] * state + get(heads, rows)

    def keep_products(i, n, terms):
        for k in range(0, AT_ONCE, 2):
            place = pl.ds(pl.multiple_of((i * AT_ONCE + k) * CHUNKS, 2 * CHUNKS), 2 * CHUNKS)
            products[place, n * LANES : (n + 1) * LANES] = jnp.concatenate(
                terms[k : k + 2], axis=0
            ).astype(BF16)

    def forward(i, carry):
        steps = [i * AT_ONCE + k for k in range(AT_ONCE)]
        rows = [pl.ds(s, CHUNKS, stride=length) for s in steps]
        a, x, g = stepped((decay, inflow, flow), rows)
        (yg,) = stepped((gx,), rows)
        for k, s in enumerate(steps):
            place = pl.ds(pl.multiple_of(s * CHUNKS, CHUNKS), CHUNKS)
            for index, value in enumerate((a, x, g, yg)):
                for t in range(count):
                    packed[index, t, place, :] = value[k][t]
        for n in range(STATE):
            b = [spread_at(spread, s, n) for s in steps]
            terms = [None] * AT_ONCE
            for t in range(count):
                h = start[t, state_at(n), :]
                for k in range(AT_ONCE):
                    h = a[k][t] * h + x[k][t] * b[k]
                    term = h * g[k][t]
                    terms[k] = term if t == 0 else terms[k] + term
                start[t, state_at(n), :] = h
            keep_products(i, n, terms)
        return carry

    lax.fori_loop(0, length // AT_ONCE, forward, 0)
    mixed[...] += jnp.dot(products[...], pick_c_ref[...], preferred_element_type=F32)
    for t in range(count):
        edge = later[t, state_at(0), :] * start[t, state_at(0), :]
        for n in range(1, STATE):
            edge = edge + later[t, state_at(n), :] * start[t, state_at(n), :]
        log_sum[t] = edge

    def backward(k, carry):
        i = length // AT_ONCE - 1 - k
        steps = [i * AT_ONCE + k for k in range(AT_ONCE)]
        places = [pl.ds(pl.multiple_of(s * CHUNKS, CHUNKS), CHUNKS) for s in steps]
        a, x, g = stepped((packed.at[0], packed.at[1], packed.at[2]), places)
        sums = [[None] * count for _ in steps]
        for n in range(STATE):
            b = [spread_at(spread, s, n) for s in steps]
            c = [spread_at(spread, s, STATE + n) for s in steps]
            terms = [None] * AT_ONCE
            for t in range(count):
                held = later[t, state_at(n), :]
                for k in range(AT_ONCE - 1, -1, -1):
                    adj = held + g[k][t] * c[k]
                    term = adj * b[k]
                    sums[k][t] = term if n == 0 else sums[k][t] + term
                    term = adj * x[k][t]
                    terms[k] = term if t == 0 else terms[k] + term
                    held = a[k][t] * adj
                later[t, state_at(n), :] = held
            keep_products(i, n, terms)
        for t in range(count):
            total = log_sum[t]
            for k in range(AT_ONCE - 1, -1, -1):
                target = pl.ds(steps[k], CHUNKS, stride=length)
                dx = sums[k][t]
                total = total + packed[3, t, places[k], :] - x[k][t] * dx
                total = jnp.where(a[k][t] == 0.0, 0.0, total)
                gx[t, target, :] = dx
                glog[t, target, :] = total
            log_sum[t] = total
        return carry

    lax.fori_loop(0, length // AT_ONCE, backward, 0)
    mixed[...] += jnp.dot(products[...], pick_b_ref[...], preferred_element_type=F32)

    @pl.when(pl.program_id(0) == pl.num_programs(0) - 1)
    def _():
        for j in range(CHUNKS):
            gbc_ref[j * length : (j + 1) * length, :] = mixed[
                pl.ds(j, length, stride=CHUNKS), :
            ].astype(BF16)

    rate = -jnp.exp(par_ref[0:1, :])
    skip = par_ref[2:3, :]
    u = u_ref[...]
    raw = pre_ref[...] + par_ref[1:2, :]
    step = softplus(raw)
    dx = get(gx, slice(None))
    dlog = get(glog, slice(None))
    gpre = (dlog * rate + dx * u) * sigmoid(raw)
    sig = sigmoid(gate)
    gu_ref[...] = (g * skip + dx * step).astype(BF16)
    gz_ref[...] = (
        grad_ref[...] * (scanned_ref[...] + skip * u) * (sig * (1.0 + gate * (1.0 - sig)))
    ).astype(BF16)
    gp_ref[...] = gpre.astype(BF16)
    gpar_ref[0:1, :] = jnp.sum(dlog * step, axis=0, keepdims=True) * rate
    gpar_ref[1:2, :] = jnp.sum(gpre, axis=0, keepdims=True)
    gpar_ref[2:3, :] = jnp.sum(g * u, axis=0, keepdims=True)
    gpar_ref[3:8, :] = jnp.zeros((5, count * LANES), F32)


class ScanCalls:
    def __init__(self, rows, wide, me):
        self.rows, self.wide, self.me = rows, wide, me
        self.length = rows // CHUNKS
        tiles = wide // LANES
        self.count = 2 if tiles % 2 == 0 else 1
        self.lanes = self.count * LANES
        self.steps = tiles // self.count
        self.bc_spec = pl.BlockSpec((rows, LANES), lambda t: (0, 3 * tiles))
        self.keep_spec = pl.BlockSpec((rows, LANES), lambda t: (0, 0))
        self.tile = pltpu.VMEM((self.count, rows, LANES), F32)
        self.thin = pltpu.VMEM((rows, LANES), F32)
        self.spread = pltpu.VMEM((rows, 2 * STATE * LANES), F32)
        self.packed = STATE * CHUNKS
        self.states = pltpu.VMEM((self.count, self.packed, LANES), F32)

    def tall(self, part):
        steps = self.steps
        return pl.BlockSpec((self.rows, self.lanes), lambda t: (0, part * steps + t))

    def flat(self, height):
        return pl.BlockSpec((height, self.lanes), lambda t: (0, t))

    def out(self, height, kind=F32):
        return jax.ShapeDtypeStruct((height, self.wide), kind)

    def call(self, kernel, in_specs, out_specs, out_shape, scratch, flops, moved):
        return pl.pallas_call(
            functools.partial(kernel, self.length, self.count),
            grid=(self.steps,),
            in_specs=[pl.BlockSpec(memory_space=pltpu.SMEM)] + in_specs,
            out_specs=out_specs,
            out_shape=out_shape,
            scratch_shapes=scratch,
            compiler_params=kernel_params(),
            cost_estimate=cost(flops, moved),
        )

    def before(self, proj, keep, par):
        return self.call(
            before_kernel,
            [self.tall(0), self.tall(2), self.bc_spec, self.keep_spec, self.flat(8)],
            [self.flat(self.packed), self.flat(CHUNKS), self.flat(STATE + 8)],
            [self.out(self.packed), self.out(CHUNKS), self.out(STATE + 8)],
            [self.tile, self.tile, self.states],
            2e9,
            self.rows * self.wide * 8,
        )(self.me, proj, proj, proj, keep, par)

    def scan(self, proj, keep, par, ends, tail, carried):
        return self.call(
            scan_kernel,
            [self.tall(0), self.tall(1), self.tall(2), self.bc_spec, self.keep_spec, self.flat(8)]
            + [self.flat(self.packed), self.flat(CHUNKS), self.flat(STATE)],
            [self.tall(0), self.tall(0), self.flat(self.packed)],
            [self.out(self.rows, BF16), self.out(self.rows), self.out(self.packed)],
            [self.spread, self.thin, self.tile, self.tile, self.tile, self.states, self.states],
            8e9,
            self.rows * self.wide * 18,
        )(self.me, proj, proj, proj, proj, keep, par, ends, tail, carried)

    def after(self, grad_mid, proj, keep, par, tail):
        return self.call(
            after_kernel,
            [self.tall(0), self.tall(1), self.tall(2), self.bc_spec, self.keep_spec, self.flat(8)]
            + [self.flat(CHUNKS)],
            [self.flat(self.packed), self.flat(STATE)],
            [self.out(self.packed), self.out(STATE)],
            [self.tile, self.tile, self.states],
            2e9,
            self.rows * self.wide * 12,
        )(self.me, grad_mid, proj, proj, proj, keep, par, tail)

    def back(self, grad_mid, proj, keep, par, tail, scanned, start, heads, carried):
        lane = jnp.arange(STATE * LANES, dtype=jnp.int32)[:, None] // LANES
        column = jnp.arange(LANES, dtype=jnp.int32)[None, :]
        pick_b = (lane == column).astype(BF16)
        pick_c = (lane + STATE == column).astype(BF16)
        pick_spec = pl.BlockSpec((STATE * LANES, LANES), lambda t: (0, 0))
        products = pltpu.VMEM((self.rows, STATE * LANES), BF16)
        return self.call(
            scan_back_kernel,
            [self.tall(0), self.tall(0), self.tall(1), self.tall(2), self.bc_spec]
            + [self.keep_spec, self.flat(8), self.flat(CHUNKS), self.tall(0)]
            + [self.flat(self.packed), self.flat(self.packed), self.flat(STATE)]
            + [pick_spec, pick_spec],
            [self.tall(0), self.tall(0), self.tall(0), self.keep_spec, self.flat(8)],
            [self.out(self.rows, BF16)] * 3
            + [jax.ShapeDtypeStruct((self.rows, LANES), BF16), self.out(8)],
            [self.spread, products] + [self.tile] * 5
            + [pltpu.VMEM((4, self.count, self.rows, LANES), F32)]
            + [self.states] * 3 + [self.thin, pltpu.VMEM((self.count, CHUNKS, LANES), F32)],
            2e10,
            self.rows * self.wide * 30,
        )(self.me, grad_mid, proj, proj, proj, proj, keep, par, tail, scanned, start, heads, carried, pick_b, pick_c)


def scores_of(base, q, keys, low_ref):
    scores = lax.dot_general(q, keys, (((1,), (1,)), ((), ())), preferred_element_type=F32)
    place = lax.broadcasted_iota(jnp.int32, scores.shape, 1) + base
    own = lax.broadcasted_iota(jnp.int32, scores.shape, 0) + (base + WINDOW)
    return jnp.where((place >= low_ref[...]) & (place <= own), scores, -1e30)


def lay_out(me_ref, block, parts, kv):
    for k, part in enumerate(parts):
        for j in range(CHUNKS):
            source = pl.multiple_of((me_ref[0] ^ j) * block, block)
            kv[(k * CHUNKS + j) * block : (k * CHUNKS + j + 1) * block, :] = part[pl.ds(source, block), :]


def attend_kernel(heads, hops, me_ref, q_ref, *refs):
    parts, (low_ref, out_ref, log_ref, kv) = refs[: hops + 1], refs[hops + 1 :]
    block = q_ref.shape[0]

    @pl.when(pl.program_id(0) == 0)
    def _():
        lay_out(me_ref, block, parts, kv)

    base = (pl.program_id(0) ^ me_ref[0]) * block + (hops * CHUNKS * block - WINDOW)
    window = pl.ds(pl.multiple_of(base, LANES), WINDOW + block)
    keys = kv[window, :LANES]
    values = kv[window, LANES:]
    lane = lax.broadcasted_iota(jnp.int32, (block, LANES), 1)
    logs = jnp.zeros((block, LANES), F32)
    for h in range(heads):
        part = slice(h * LANES, (h + 1) * LANES)
        scores = scores_of(base, q_ref[:, part], keys, low_ref)
        top = jnp.max(scores, axis=1, keepdims=True)
        soft = jnp.exp(scores - top)
        total = jnp.sum(soft, axis=1, keepdims=True)
        mix = jnp.dot(soft.astype(BF16), values, preferred_element_type=F32)
        out_ref[:, part] = (mix * (1.0 / total)).astype(BF16)
        logs = jnp.where(lane == h, top + jnp.log(total), logs)
    log_ref[...] = logs


def attend_back_kernel(heads, hops, me_ref, q_ref, *refs):
    parts, refs = refs[: hops + 1], refs[hops + 1 :]
    low_ref, log_ref, grad_ref, gq_ref = refs[:4]
    gparts, (kv, gkv) = refs[4 : hops + 5], refs[hops + 5 :]
    block = q_ref.shape[0]

    @pl.when(pl.program_id(0) == 0)
    def _():
        lay_out(me_ref, block, parts, kv)
        gkv[...] = jnp.zeros_like(gkv)

    base = (pl.program_id(0) ^ me_ref[0]) * block + (hops * CHUNKS * block - WINDOW)
    window = pl.ds(pl.multiple_of(base, LANES), WINDOW + block)
    keys = kv[window, :LANES]
    values = kv[window, LANES:]
    turned = (((0,), (0,)), ((), ()))
    for h in range(heads):
        part = slice(h * LANES, (h + 1) * LANES)
        q = q_ref[:, part]
        grad = grad_ref[:, part]
        soft = jnp.exp(scores_of(base, q, keys, low_ref) - log_ref[:, h : h + 1])
        gsoft = lax.dot_general(grad, values, (((1,), (1,)), ((), ())), preferred_element_type=F32)
        delta = jnp.sum(soft * gsoft, axis=1, keepdims=True)
        gscore = (soft * (gsoft - delta)).astype(BF16)
        gq_ref[:, part] = (
            jnp.dot(gscore, keys, preferred_element_type=F32) * 0.125
        ).astype(BF16)
        gkv[window, :LANES] += lax.dot_general(gscore, q, turned, preferred_element_type=F32)
        gkv[window, LANES:] += lax.dot_general(
            soft.astype(BF16), grad, turned, preferred_element_type=F32
        )

    @pl.when(pl.program_id(0) == pl.num_programs(0) - 1)
    def _():
        for k, part in enumerate(gparts):
            for j in range(CHUNKS):
                target = pl.multiple_of((me_ref[0] ^ j) * block, block)
                part[pl.ds(target, block), :] = gkv[
                    (k * CHUNKS + j) * block : (k * CHUNKS + j + 1) * block, :
                ].astype(part.dtype)


def attend_specs(rows, hops):
    block = rows // CHUNKS
    by_row = lambda width: pl.BlockSpec((block, width), lambda b: (b, 0))
    whole = [pl.BlockSpec((rows, 2 * LANES), lambda b: (0, 0))] * (hops + 1)
    total = (hops + 1) * rows
    return by_row, whole, total, pl.BlockSpec(memory_space=pltpu.SMEM)


def attend(me, q, kvs, low):
    rows, wide = q.shape
    heads = wide // LANES
    by_row, whole, total, scalar = attend_specs(rows, len(kvs) - 1)
    return pl.pallas_call(
        functools.partial(attend_kernel, heads, len(kvs) - 1),
        grid=(CHUNKS,),
        in_specs=[scalar, by_row(wide), *whole, by_row(1)],
        out_specs=[by_row(wide), by_row(LANES)],
        out_shape=[
            jax.ShapeDtypeStruct((rows, wide), BF16),
            jax.ShapeDtypeStruct((rows, LANES), F32),
        ],
        scratch_shapes=[pltpu.VMEM((total, 2 * LANES), BF16)],
        compiler_params=kernel_params(),
        cost_estimate=cost(6e9, 8e6),
    )(me, q, *kvs, low)


def attend_back(me, q, kvs, low, logs, grad):
    rows, wide = q.shape
    heads = wide // LANES
    by_row, whole, total, scalar = attend_specs(rows, len(kvs) - 1)
    part = jax.ShapeDtypeStruct((rows, 2 * LANES), BF16)
    own = jax.ShapeDtypeStruct((rows, 2 * LANES), F32)
    return pl.pallas_call(
        functools.partial(attend_back_kernel, heads, len(kvs) - 1),
        grid=(CHUNKS,),
        in_specs=[scalar, by_row(wide), *whole, by_row(1), by_row(LANES), by_row(wide)],
        out_specs=[by_row(wide), *whole],
        out_shape=[jax.ShapeDtypeStruct((rows, wide), BF16)] + [part] * (len(kvs) - 1) + [own],
        scratch_shapes=[
            pltpu.VMEM((total, 2 * LANES), BF16),
            pltpu.VMEM((total, 2 * LANES), F32),
        ],
        compiler_params=kernel_params(),
        cost_estimate=cost(1.5e10, 1.2e7),
    )(me, q, *kvs, low, logs, grad)


def swap_cores(value):
    return lax.ppermute(value, "core", [(0, 1), (1, 0)])


def from_peer(value, k):
    return lax.ppermute(value, "tp", [(n, n ^ k) for n in range(lax.axis_size("tp"))])


def team_gather(rows):
    tps = lax.axis_size("tp")
    got = {k: from_peer(rows, k) for k in range(tps - 1, 0, -1)}
    own = jnp.concatenate([rows] + [got[k] for k in range(1, tps)], axis=0)
    return jnp.concatenate([own, swap_cores(own)], axis=0)


def team_scatter(values):
    tps = lax.axis_size("tp")
    half = values.shape[0] // CORES
    block = half // tps
    both = values[:half].astype(F32) + swap_cores(values[half:]).astype(F32)
    low = both.astype(BF16)
    got = [from_peer(low[k * block : (k + 1) * block], k) for k in range(tps - 1, 0, -1)]
    total = both[:block]
    for part in got:
        total = total + part.astype(F32)
    return total


def shifted(value, steps):
    count = lax.axis_size("chip")
    leading, last = (max(0, -steps), min(count, count - steps))
    return lax.ppermute(value, "chip", [(k, k + steps) for k in range(leading, last)])


def behind(value, other):
    first = other[(slice(0, 1),) * other.ndim].reshape((1,) * value.ndim)
    return value + (first * 0).astype(value.dtype)


def by_core(mine, other):
    first = lax.axis_index("core") == 0
    return jnp.where(first, mine, other), jnp.where(first, other, mine)


def to_rows(values):
    tps = lax.axis_size("tp")
    half = values.shape[0] // CORES
    block = half // tps
    pair = jnp.concatenate([values[:half], swap_cores(values[half:])], axis=1)
    got = [from_peer(pair[k * block : (k + 1) * block], k) for k in range(1, tps)]
    return jnp.concatenate([pair[:block]] + got, axis=1)


def to_columns(values):
    tps = lax.axis_size("tp")
    step = values.shape[1] // tps
    got = [from_peer(values[:, k * step : (k + 1) * step], k) for k in range(1, tps)]
    pair = jnp.concatenate([values[:, :step]] + got, axis=0)
    return jnp.concatenate([pair[:, : step // CORES], swap_cores(pair[:, step // CORES :])], axis=0)


def own_halves(shard, other=None):
    core = lax.axis_index("core")
    if other is not None:
        shard = behind(shard, other)
    mine = lax.dynamic_index_in_dim(shard, core, 1, False)
    other = swap_cores(lax.dynamic_index_in_dim(shard, 1 - core, 1, False))
    pair = jnp.concatenate(by_core(mine, other), axis=0)
    return lax.all_gather(pair, "chip", axis=0, tiled=True)


def summed_halves(full):
    rows = lax.psum_scatter(full, "chip", scatter_dimension=0, tiled=True)
    rows = rows.reshape(CORES, rows.shape[0] // CORES, -1)
    core = lax.axis_index("core")
    mine = lax.dynamic_index_in_dim(rows, core, 0, False)
    return mine, swap_cores(lax.dynamic_index_in_dim(rows, 1 - core, 0, False))


def share_columns(mine, other):
    tps = lax.axis_size("tp")
    pair = jnp.stack([mine, other])
    whole = jnp.concatenate([pair] + [from_peer(pair, k) for k in range(1, tps)], axis=0)
    own = lax.axis_index("tp") * CORES + lax.axis_index("core")
    return jnp.concatenate(
        [lax.dynamic_slice_in_dim(whole, own ^ k, 1, 0) for k in range(CORES * tps)], axis=0
    )


def body(
    x_in, lengths, w_q, w_kv, w_o, input_weight, a_log, dt_bias, d_skip,
    w_bc, w_out, gains, gate_up_weight, w_down, cotangent,
):
    chips, tps = lax.axis_size("chip"), lax.axis_size("tp")
    chip, core, tp = (lax.axis_index(name) for name in ("chip", "core", "tp"))
    team = CORES * tps
    unit = tp * CORES + core
    layers, shard_rows, width = w_q.shape
    rows_own = x_in.shape[0]
    rows = rows_own * team
    hops = -(-WINDOW // rows)
    kv_half = w_kv.shape[2] // 2
    heads_here = -(-HEADS // team)
    q_wide = heads_here * HEAD
    slot_wide = SLOTS * HEAD
    channels = a_log.shape[1] // CORES
    wide = round_up(channels, LANES)
    hidden_here = gate_up_weight.shape[3] // CORES
    out_wide = round_up(channels + width // CORES, LANES)
    ffn_wide = round_up(3 * hidden_here, LANES)
    me = (core * tps + tp).astype(jnp.int32)
    me_array = jnp.reshape(me, (1,))
    scan = ScanCalls(rows, wide, me_array)

    order = jnp.arange(team, dtype=jnp.int32) ^ me
    local = order[:, None] * rows_own + jnp.arange(rows_own, dtype=jnp.int32)[None, :]
    places = chip * rows + local.reshape(rows)
    starts = (jnp.cumsum(lengths) - lengths).astype(jnp.int32)
    reached = places[:, None] >= starts[None, :]
    opening = jnp.any(places[:, None] == starts[None, :], axis=1)
    keep = jnp.broadcast_to((1.0 - opening.astype(F32))[:, None], (rows, LANES))
    first = jnp.max(jnp.where(reached, starts[None, :], 0), axis=1)
    low = jnp.maximum(first, places - (WINDOW - 1)) - (chip - hops) * rows
    low = low[:, None]

    head_ids = unit * heads_here + jnp.arange(heads_here, dtype=jnp.int32)
    slot_ids = head_ids // GROUP - (unit * heads_here) // GROUP
    upper = (slot_ids == 1)[None, :, None]

    def pad_lanes(values, size):
        return jnp.pad(values, [(0, 0)] * (values.ndim - 1) + [(0, size - values.shape[-1])])

    def kv_columns(layer, index):
        base = (index * heads_here) // GROUP * HEAD
        whole = jnp.pad(w_kv[layer].reshape(shard_rows, 2, kv_half), ((0, 0), (0, 0), (0, slot_wide)))
        return lax.dynamic_slice_in_dim(whole, base, slot_wide, 2).reshape(shard_rows, 2 * slot_wide)

    def fetch_mixer_in(layer, lead=None):
        ins = input_weight[layer].reshape(shard_rows, 3, CORES, channels)
        ins = pad_lanes(ins.transpose(0, 2, 1, 3), wide).reshape(shard_rows, CORES, 3 * wide)
        qs = lax.dynamic_slice_in_dim(
            pad_lanes(w_q[layer], team * q_wide), tp * CORES * q_wide, CORES * q_wide, 1
        ).reshape(shard_rows, CORES, q_wide)
        kvs = jnp.stack([kv_columns(layer, tp * CORES + k) for k in range(CORES)], axis=1)
        full = own_halves(jnp.concatenate([ins, qs, kvs], axis=2), lead)
        return full[:, 3 * wide :], full[:, : 3 * wide]

    def fetch_mixer_out(layer, lead):
        outs = pad_lanes(w_out[layer].T.reshape(shard_rows, CORES, channels), wide)
        os = w_o[layer].reshape(shard_rows, CORES, width // CORES)
        os = pad_lanes(os, round_up(width // CORES, LANES))
        full = own_halves(jnp.concatenate([outs, os], axis=2), lead)
        o = jnp.pad(full[:, wide : wide + width // CORES], ((0, team * q_wide - width), (0, 0)))
        o = jnp.concatenate(
            [lax.dynamic_slice_in_dim(o, (unit ^ k) * q_wide, q_wide, 0) for k in range(team)], axis=0
        )
        blocks = swap_cores(o).reshape(tps, CORES, q_wide, -1)
        blocks = blocks[:, ::-1].reshape(o.shape)
        return full[:, :wide], jnp.concatenate(by_core(o, blocks), axis=1)

    def fetch_ffn(layer, lead):
        gus = gate_up_weight[layer].reshape(shard_rows, 2, CORES, hidden_here)
        gus = gus.transpose(0, 2, 1, 3).reshape(shard_rows, CORES, 2 * hidden_here)
        downs = w_down[layer].T.reshape(shard_rows, CORES, hidden_here)
        full = own_halves(pad_lanes(jnp.concatenate([gus, downs], axis=2), ffn_wide), lead)
        return full[:, : 2 * hidden_here], full[:, 2 * hidden_here : 3 * hidden_here]

    def scan_params(layer):
        mine = [
            lax.dynamic_slice_in_dim(part[layer], core * channels, channels, 0)
            for part in (a_log, dt_bias, d_skip)
        ]
        return jnp.pad(jnp.stack(mine), ((0, 5), (0, wide - channels)))

    def chain(everything, back):
        state = jnp.zeros(everything[0][0].shape, F32)
        order = range(chips - 1, -1, -1) if back else range(chips)
        for k in order:
            counts = (k > chip) if back else (k < chip)
            new = everything[1][k][None, :] * state + everything[0][k]
            state = jnp.where(counts, new, state)
        return state

    def slots(values):
        values = values.reshape(rows, heads_here, HEAD)
        nothing = jnp.zeros_like(values)
        return jnp.concatenate(
            [jnp.where(upper, nothing, values), jnp.where(upper, values, nothing)], axis=2
        ).reshape(rows, heads_here * slot_wide)

    def unslot(values):
        values = values.reshape(rows, heads_here, SLOTS, HEAD)
        return jnp.where(upper, values[:, :, 1], values[:, :, 0]).reshape(rows, q_wide)

    def forward_layer(stream, layer, weights):
        (w_attn, w_ssm), (w_mamba, w_attn_out), (w_gu, w_dn) = weights
        gain = gains[layer]
        par = scan_params(layer)
        normed = rms_scale(stream, gain[0]).astype(BF16)
        normed_all = team_gather(normed)
        qkv = dot(normed_all, w_attn, BF16)
        kv = qkv[:, q_wide:]
        kvs = [shifted(kv, hop) for hop in range(hops, 0, -1)] + [kv]
        bc = dot(normed_all, pad_lanes(w_bc[layer], LANES), BF16).astype(F32)
        proj = jnp.concatenate([dot(normed_all, w_ssm), bc], axis=1)
        ends, tail, dev = scan.before(proj, keep, par)
        devs = lax.all_gather(dev, "chip")
        chip_decay = devs[:, STATE]
        carried = chain((devs[:, :STATE], chip_decay), False)
        q = slots(qkv[:, :q_wide] * BF16(0.125))
        mix, logs = attend(me_array, q, kvs, low)
        attended = unslot(mix)
        attn_out = dot(to_rows(attended), w_attn_out)
        mid, scanned, start = scan.scan(proj, keep, behind(par, attended), ends, tail, carried)
        mamba_out = team_scatter(dot_nt(mid, w_mamba, BF16))
        middle = stream + branch_mix(attn_out, mamba_out, gain[1], gain[2])
        ffn_all = team_gather(rms_scale(middle, gain[3]).astype(BF16))
        gate_up = dot(ffn_all, w_gu)
        hidden = swiglu(gate_up).astype(BF16)
        ffn_out = team_scatter(dot_nt(hidden, w_dn, BF16))
        kept = dict(
            stream=stream, normed_all=normed_all, q=q, kvs=kvs, logs=logs,
            attended=attended, proj=proj, tail=tail, chip_decay=chip_decay, mid=mid,
            scanned=scanned, start=start, attn_out=attn_out, mamba_out=mamba_out, middle=middle,
            ffn_all=ffn_all, gate_up=gate_up, hidden=hidden, par=par,
        )
        return middle + ffn_out, kept

    def backward_layer(grad_out, layer, weights, kept):
        (w_attn, w_ssm), (w_mamba, w_attn_out), (w_gu, w_dn) = weights
        gain = gains[layer]
        normed_all = kept["normed_all"]
        grad_all = team_gather(grad_out.astype(BF16))
        grad_hidden = dot(grad_all, w_dn)
        _, swiglu_pull = jax.vjp(swiglu, kept["gate_up"])
        grad_gu = swiglu_pull(grad_hidden)[0].astype(BF16)
        grad_ffn = team_scatter(dot_nt(grad_gu, w_gu, BF16))
        ffn_sums = summed_halves(
            pad_lanes(
                jnp.concatenate(
                    [dot_tn(kept["ffn_all"], grad_gu, BF16), dot_tn(grad_all, kept["hidden"], BF16)],
                    axis=1,
                ),
                ffn_wide,
            )
        )
        _, norm_pull = jax.vjp(rms_scale, kept["middle"], gain[3])
        grad_mid_norm, grad_gain_ffn = norm_pull(grad_ffn)
        grad_middle = grad_out + grad_mid_norm
        _, mix_pull = jax.vjp(branch_mix, kept["attn_out"], kept["mamba_out"], gain[1], gain[2])
        grad_attn, grad_mamba, grad_gain_attn, grad_gain_mamba = mix_pull(grad_middle)
        grad_mamba_all = team_gather(grad_mamba.astype(BF16))
        grad_attn = grad_attn.astype(BF16)
        grad_att = slots(to_columns(dot_nt(grad_attn, w_attn_out, BF16)))
        grad_attn_all = team_gather(behind(grad_attn, grad_mamba_all))
        grad_mid = dot(grad_mamba_all, w_mamba)
        par = kept["par"]
        heads, dev = scan.after(grad_mid, kept["proj"], keep, par, kept["tail"])
        devs = lax.all_gather(dev, "chip")
        carried = chain((devs, kept["chip_decay"]), True)

        gq, *gkvs = attend_back(me_array, kept["q"], kept["kvs"], low, kept["logs"], grad_att)
        gkv = gkvs[hops]
        for hop in range(1, hops + 1):
            gkv = gkv + shifted(gkvs[hops - hop], -hop).astype(F32)
        grad_qkv = jnp.concatenate([unslot(gq), gkv.astype(BF16)], axis=1)
        attn_sums = summed_halves(
            jnp.concatenate(
                [
                    dot_tn(grad_mamba_all, kept["mid"], BF16),
                    dot_tn(grad_attn_all, kept["attended"], BF16),
                    dot_tn(normed_all, grad_qkv, BF16),
                ],
                axis=1,
            )
        )
        gu, gz, gp, gbc, gpar = scan.back(
            grad_mid, kept["proj"], keep, par, kept["tail"], kept["scanned"], kept["start"], heads, carried
        )
        grad_proj = jnp.concatenate([gu, gz, gp, gbc], axis=1)
        grad_normed = team_scatter(
            (
                dot_nt(grad_qkv, w_attn)
                + dot_nt(grad_proj[:, : 3 * wide], w_ssm)
                + dot_nt(gbc, pad_lanes(w_bc[layer], LANES))
            ).astype(BF16)
        )
        ssm_sums = summed_halves(dot_tn(normed_all, grad_proj, BF16))
        _, in_pull = jax.vjp(rms_scale, kept["stream"], gain[0])
        grad_stream_norm, grad_gain_in = in_pull(grad_normed)
        grad_gains = jnp.stack([grad_gain_in, grad_gain_attn, grad_gain_mamba, grad_gain_ffn])
        shared = share_columns(*(part[:, wide:] for part in attn_sums))
        shared_bc = share_columns(*(part[:, 3 * wide :] for part in ssm_sums))
        small = jnp.concatenate([grad_gains.reshape(-1), gpar[:3, :channels].reshape(-1)])
        return grad_middle + grad_stream_norm, (ffn_sums, attn_sums, ssm_sums, shared, shared_bc, small)

    weights = []
    lead = None
    for layer in range(layers):
        ins = fetch_mixer_in(layer, lead)
        lead = ins[0] if layer == 0 else lead
        weights.append((ins, fetch_mixer_out(layer, lead), fetch_ffn(layer, lead)))
    stream = x_in.astype(F32)
    kept = []
    for layer in range(layers):
        stream, saved = forward_layer(stream, layer, weights[layer])
        kept.append(saved)
    block_out = stream.astype(BF16)
    grad_stream = cotangent.astype(F32)
    sums = [None] * layers
    for layer in range(layers - 1, -1, -1):
        grad_stream, sums[layer] = backward_layer(grad_stream, layer, weights[layer], kept[layer])

    shared = jnp.stack([parts[3] for parts in sums]).transpose(0, 2, 1, 3)
    turned = shared[..., :q_wide].reshape(layers, shard_rows, team * q_wide)[..., :width]
    grad_o = lax.all_to_all(turned, ("chip", "core"), split_axis=2, concat_axis=1, tiled=True)
    grad_o = grad_o.transpose(0, 2, 1).astype(F32)
    grad_q = shared[..., q_wide : 2 * q_wide].reshape(layers, shard_rows, team * q_wide)
    grad_q = grad_q[..., :width].astype(F32)
    kv_parts = shared[..., 2 * q_wide :].astype(F32)
    kv_parts = kv_parts.reshape(layers, shard_rows, team, 2, SLOTS, HEAD)
    kv_heads = []
    for head in range(KV_HEADS):
        terms = [
            kv_parts[:, :, k, :, slot]
            for k in range(team)
            for slot in range(SLOTS)
            if (k * heads_here) // GROUP + slot == head
        ]
        kv_heads.append(sum(terms[1:], terms[0]))
    grad_kv = jnp.stack(kv_heads, axis=3).reshape(layers, shard_rows, 2 * kv_half)
    grad_bc = jnp.stack([jnp.sum(parts[4].astype(F32), axis=0) for parts in sums])[..., : 2 * STATE]

    def halves(which, begin, end):
        return [
            jnp.stack(by_core(*(part[:, begin:end] for part in parts[which]))).astype(F32)
            for parts in sums
        ]

    grad_in = jnp.stack(
        [
            pair.reshape(CORES, shard_rows, 3, wide)[..., :channels]
            .transpose(1, 2, 0, 3)
            .reshape(shard_rows, 3, CORES * channels)
            for pair in halves(2, 0, 3 * wide)
        ]
    )
    grad_out = jnp.stack(
        [
            pair.transpose(0, 2, 1).reshape(CORES * channels, shard_rows)
            for pair in halves(1, 0, channels)
        ]
    )
    grad_gu = jnp.stack(
        [
            pair.reshape(CORES, shard_rows, 2, hidden_here)
            .transpose(1, 2, 0, 3)
            .reshape(shard_rows, 2, CORES * hidden_here)
            for pair in halves(0, 0, 2 * hidden_here)
        ]
    )
    grad_down = jnp.stack(
        [
            pair.transpose(0, 2, 1).reshape(CORES * hidden_here, shard_rows)
            for pair in halves(0, 2 * hidden_here, 3 * hidden_here)
        ]
    )
    small = jnp.sum(lax.all_gather(jnp.stack([parts[5] for parts in sums]), "chip"), axis=0)
    small = share_columns(small, swap_cores(small))
    place = chip * CORES + core
    gain_full = jnp.sum(small[..., : 4 * width], axis=0).reshape(layers, 4, width)
    grad_gains = lax.dynamic_slice_in_dim(gain_full, place * shard_rows, shard_rows, 2)
    ssm_full = small[..., 4 * width :].reshape(team, layers, 3, channels)
    ssm_full = ssm_full.transpose(1, 2, 0, 3).reshape(layers, 3, team * channels)
    share = team * channels // (chips * CORES)
    ssm_own = lax.dynamic_slice_in_dim(ssm_full, place * share, share, 2)
    return (
        block_out, grad_stream, grad_q, grad_kv, grad_o, grad_in,
        ssm_own[:, 0], ssm_own[:, 1], ssm_own[:, 2], grad_bc, grad_out, grad_gains, grad_gu, grad_down,
    )


def solution(mesh):
    fsdp, tp = mesh.shape["fsdp"], mesh.shape["tp"]
    inner = Mesh(mesh.devices.reshape(fsdp // CORES, CORES, tp), ("chip", "core", "tp"))
    shards = ("chip", "core")
    tokens = P(("chip", "core", "tp"), None)
    by_row = P(None, shards, None)
    return jax.shard_map(
        body,
        mesh=inner,
        in_specs=(
            tokens, P(), by_row, by_row, by_row, P(None, shards, None, "tp"),
            P(None, "tp"), P(None, "tp"), P(None, "tp"), P(), P(None, "tp", shards), P(),
            P(None, shards, None, "tp"), P(None, "tp", shards), tokens,
        ),
        out_specs=(
            tokens, tokens, by_row, by_row, by_row, P(None, shards, None, "tp"),
            P(None, shards), P(None, shards), P(None, shards), by_row, P(None, "tp", shards),
            P(None, None, shards), P(None, shards, None, "tp"), P(None, "tp", shards),
        ),
        check_vma=False,
    )
```

```python
import functools

import jax
import jax.numpy as jnp
from jax import lax
from jax.experimental import pallas as pl
from jax.experimental.pallas import tpu as pltpu
from jax.sharding import Mesh
from jax.sharding import PartitionSpec as P

HEADS = 25
HEAD = 64
KV_HEADS = 5
GROUP = HEADS // KV_HEADS
WINDOW = 1024
STATE = 16
EPSILON = 1e-05
TOP_PRECISION = lax.Precision.HIGHEST

CORES = 2
CHUNKS = 8
AT_ONCE = 4
LANES = 128
SLOTS = 2
VMEM_BYTES = 56 * 1024 * 1024
F32 = jnp.float32
BF16 = jnp.bfloat16


def round_up(value, unit):
    return -(-value // unit) * unit


def dot(a, b, out=F32):
    return jnp.dot(a, b, preferred_element_type=F32).astype(out)


def dot_nt(a, b, out=F32):
    return lax.dot_general(
        a, b, (((1,), (1,)), ((), ())), preferred_element_type=F32
    ).astype(out)


def dot_tn(a, b, out=F32):
    return lax.dot_general(
        a, b, (((0,), (0,)), ((), ())), preferred_element_type=F32
    ).astype(out)


def rms_scale(count, values, gain_row):
    mean = jnp.sum(values * values, axis=-1, keepdims=True) / count
    return values * lax.rsqrt(mean + EPSILON) * gain_row


def branch_mix(count, attn_out, mamba_out, gain_attn, gain_mamba):
    return 0.5 * (
        rms_scale(count, attn_out, gain_attn) + rms_scale(count, mamba_out, gain_mamba)
    )


def swiglu(gate_up_product):
    half = gate_up_product.shape[1] // 2
    return jax.nn.silu(gate_up_product[:, :half]) * gate_up_product[:, half:]


def softplus(v):
    return jnp.maximum(v, 0.0) + jnp.log1p(jnp.exp(-jnp.abs(v)))


def sigmoid(v):
    return 1.0 / (1.0 + jnp.exp(-v))


def kernel_params(bytes_limit=VMEM_BYTES):
    return pltpu.CompilerParams(
        dimension_semantics=("arbitrary",), vmem_limit_bytes=bytes_limit
    )


def cost(flops, moved):
    return pl.CostEstimate(flops=int(flops), bytes_accessed=int(moved), transcendentals=0)


def spread_bc(bc_ref, spread, turned, length):
    def turn(s, carry):
        place = pl.ds(pl.multiple_of(s * CHUNKS, CHUNKS), CHUNKS)
        turned[place, :] = bc_ref[pl.ds(s, CHUNKS, stride=length), :]
        return carry

    lax.fori_loop(0, length, turn, 0, unroll=8)
    block = 2 * LANES
    for q in range(2 * STATE * LANES // block):
        row = lax.broadcasted_iota(jnp.int32, (LANES, block), 0)
        column = lax.broadcasted_iota(jnp.int32, (LANES, block), 1) + q * block
        pick = (row == column // LANES).astype(F32).astype(BF16)
        for r in range(CHUNKS * length // block):
            part = slice(r * block, (r + 1) * block)
            spread[part, q * block : (q + 1) * block] = jnp.dot(
                turned[part, :].astype(BF16), pick, preferred_element_type=F32
            )


def spread_at(spread, s, n):
    place = pl.ds(pl.multiple_of(s * CHUNKS, CHUNKS), CHUNKS)
    return spread[place, n * LANES : (n + 1) * LANES]


def wide_lanes(t):
    return slice(t * LANES, (t + 1) * LANES)


def put(ref, value):
    for t in range(ref.shape[0]):
        ref[t] = value[:, wide_lanes(t)]


def get(ref, rows):
    return jnp.concatenate([ref[t, rows, :] for t in range(ref.shape[0])], axis=1)


def put_rows(ref, rows, value):
    for t in range(ref.shape[0]):
        ref[t, rows, :] = value[:, wide_lanes(t)]


def fill_decay(u_ref, pre_ref, keep_ref, par_ref, decay, inflow, count):
    step = softplus(pre_ref[...] + par_ref[1:2, :])
    keep = jnp.concatenate([keep_ref[...]] * count, axis=1)
    put(decay, jnp.exp(-step * jnp.exp(par_ref[0:1, :])) * keep)
    if u_ref is not None:
        put(inflow, step * u_ref[...])


def state_at(n):
    return slice(n * CHUNKS, (n + 1) * CHUNKS)


def stepped(refs, rows):
    return [[[ref[t, part, :] for t in range(ref.shape[0])] for part in rows] for ref in refs]


def before_kernel(length, count, me_ref, u_ref, pre_ref, bc_ref, keep_ref, par_ref, ends_ref, tail_ref, dev_ref, decay, inflow, ends):
    fill_decay(u_ref, pre_ref, keep_ref, par_ref, decay, inflow, count)

    def walk(k, rest):
        rows = pl.ds(length - 1 - k, CHUNKS, stride=length)
        for t in range(count):
            inflow[t, rows, :] = inflow[t, rows, :] * rest[t]
        return tuple(rest[t] * decay[t, rows, :] for t in range(count))

    ones = jnp.ones((CHUNKS, LANES), F32)
    rest = lax.fori_loop(0, length, walk, (ones,) * count, unroll=8)
    tail_ref[...] = jnp.concatenate(rest, axis=1)
    for r in range(CHUNKS):
        part = pl.ds(r * length, length)
        end = lax.dot_general(
            bc_ref[part, :].astype(BF16),
            get(inflow, part).astype(BF16),
            (((0,), (0,)), ((), ())),
            preferred_element_type=F32,
        )
        put_rows(ends, pl.ds(r, STATE, stride=CHUNKS), end[:STATE])
    ends_ref[...] = get(ends, slice(None))
    state = jnp.zeros((STATE, count * LANES), F32)
    total = jnp.ones((1, count * LANES), F32)
    for j in range(CHUNKS):
        r = me_ref[0] ^ j
        fade = tail_ref[pl.ds(r, 1), :]
        state = fade * state + get(ends, pl.ds(r, STATE, stride=CHUNKS))
        total = total * fade
    dev_ref[0:STATE, :] = state
    dev_ref[STATE : STATE + 8, :] = jnp.broadcast_to(total, (8, count * LANES))


def scan_kernel(
    length, count, me_ref, u_ref, gate_ref, pre_ref, bc_ref, keep_ref, par_ref, ends_ref, tail_ref, carried_ref,
    mid_ref, scanned_ref, start_ref, spread, turned, decay, inflow, scanned, ends, start,
):
    @pl.when(pl.program_id(0) == 0)
    def _():
        spread_bc(bc_ref, spread, turned, length)

    fill_decay(u_ref, pre_ref, keep_ref, par_ref, decay, inflow, count)
    put(ends, ends_ref[...])
    state = carried_ref[...]
    for j in range(CHUNKS):
        r = me_ref[0] ^ j
        rows = pl.ds(r, STATE, stride=CHUNKS)
        put_rows(start, rows, state)
        state = tail_ref[pl.ds(r, 1), :] * state + get(ends, rows)
    start_ref[...] = get(start, slice(None))

    def walk(i, carry):
        steps = [i * AT_ONCE + k for k in range(AT_ONCE)]
        rows = [pl.ds(s, CHUNKS, stride=length) for s in steps]
        a, x = stepped((decay, inflow), rows)
        sums = [[None] * count for _ in steps]
        for n in range(STATE):
            b = [spread_at(spread, s, n) for s in steps]
            c = [spread_at(spread, s, STATE + n) for s in steps]
            for t in range(count):
                h = start[t, state_at(n), :]
                for k in range(AT_ONCE):
                    h = a[k][t] * h + x[k][t] * b[k]
                    term = h * c[k]
                    sums[k][t] = term if n == 0 else sums[k][t] + term
                start[t, state_at(n), :] = h
        for k, part in enumerate(rows):
            for t in range(count):
                scanned[t, part, :] = sums[k][t]
        return carry

    lax.fori_loop(0, length // AT_ONCE, walk, 0)
    gate = gate_ref[...]
    y = get(scanned, slice(None))
    scanned_ref[...] = y
    mid_ref[...] = ((y + par_ref[2:3, :] * u_ref[...]) * (gate * sigmoid(gate))).astype(BF16)


def after_kernel(length, count, me_ref, grad_ref, gate_ref, pre_ref, bc_ref, keep_ref, par_ref, tail_ref, heads_ref, dev_ref, decay, flow, heads):
    fill_decay(None, pre_ref, keep_ref, par_ref, decay, None, count)
    gate = gate_ref[...]
    put(flow, grad_ref[...] * (gate * sigmoid(gate)))

    def walk(s, run):
        rows = pl.ds(s, CHUNKS, stride=length)
        new = []
        for t in range(count):
            new.append(run[t] * decay[t, rows, :])
            flow[t, rows, :] = flow[t, rows, :] * new[t]
        return tuple(new)

    lax.fori_loop(0, length, walk, (jnp.ones((CHUNKS, LANES), F32),) * count, unroll=8)
    for r in range(CHUNKS):
        part = pl.ds(r * length, length)
        head = lax.dot_general(
            bc_ref[part, :].astype(BF16),
            get(flow, part).astype(BF16),
            (((0,), (0,)), ((), ())),
            preferred_element_type=F32,
        )
        put_rows(heads, pl.ds(r, STATE, stride=CHUNKS), head[STATE : 2 * STATE])
    heads_ref[...] = get(heads, slice(None))
    state = jnp.zeros((STATE, count * LANES), F32)
    for j in range(CHUNKS - 1, -1, -1):
        r = me_ref[0] ^ j
        state = tail_ref[pl.ds(r, 1), :] * state + get(heads, pl.ds(r, STATE, stride=CHUNKS))
    dev_ref[...] = state


def scan_back_kernel(
    length, count, me_ref, grad_ref, u_ref, gate_ref, pre_ref, bc_ref, keep_ref, par_ref, tail_ref, scanned_ref, start_ref,
    heads_ref, carried_ref, pick_b_ref, pick_c_ref,
    gu_ref, gz_ref, gp_ref, gbc_ref, gpar_ref,
    spread, products, decay, inflow, flow, gx, glog, packed, later, heads, start, mixed, log_sum,
):
    @pl.when(pl.program_id(0) == 0)
    def _():
        spread_bc(bc_ref, spread, mixed, length)
        mixed[...] = jnp.zeros_like(mixed)

    fill_decay(u_ref, pre_ref, keep_ref, par_ref, decay, inflow, count)
    gate = gate_ref[...]
    g = grad_ref[...] * (gate * sigmoid(gate))
    put(flow, g)
    put(gx, g * scanned_ref[...])
    put(heads, heads_ref[...])
    put(start, start_ref[...])
    state = carried_ref[...]
    for j in range(CHUNKS - 1, -1, -1):
        r = me_ref[0] ^ j
        rows = pl.ds(r, STATE, stride=CHUNKS)
        put_rows(later, rows, state)
        state = tail_ref[pl.ds(r, 1), :] * state + get(heads, rows)

    def keep_products(i, n, terms):
        for k in range(0, AT_ONCE, 2):
            place = pl.ds(pl.multiple_of((i * AT_ONCE + k) * CHUNKS, 2 * CHUNKS), 2 * CHUNKS)
            products[place, n * LANES : (n + 1) * LANES] = jnp.concatenate(
                terms[k : k + 2], axis=0
            ).astype(BF16)

    def forward(i, carry):
        steps = [i * AT_ONCE + k for k in range(AT_ONCE)]
        rows = [pl.ds(s, CHUNKS, stride=length) for s in steps]
        a, x, g = stepped((decay, inflow, flow), rows)
        (yg,) = stepped((gx,), rows)
        for k, s in enumerate(steps):
            place = pl.ds(pl.multiple_of(s * CHUNKS, CHUNKS), CHUNKS)
            for index, value in enumerate((a, x, g, yg)):
                for t in range(count):
                    packed[index, t, place, :] = value[k][t]
        for n in range(STATE):
            b = [spread_at(spread, s, n) for s in steps]
            terms = [None] * AT_ONCE
            for t in range(count):
                h = start[t, state_at(n), :]
                for k in range(AT_ONCE):
                    h = a[k][t] * h + x[k][t] * b[k]
                    term = h * g[k][t]
                    terms[k] = term if t == 0 else terms[k] + term
                start[t, state_at(n), :] = h
            keep_products(i, n, terms)
        return carry

    lax.fori_loop(0, length // AT_ONCE, forward, 0)
    mixed[...] += jnp.dot(products[...], pick_c_ref[...], preferred_element_type=F32)
    for t in range(count):
        edge = later[t, state_at(0), :] * start[t, state_at(0), :]
        for n in range(1, STATE):
            edge = edge + later[t, state_at(n), :] * start[t, state_at(n), :]
        log_sum[t] = edge

    def backward(k, carry):
        i = length // AT_ONCE - 1 - k
        steps = [i * AT_ONCE + k for k in range(AT_ONCE)]
        places = [pl.ds(pl.multiple_of(s * CHUNKS, CHUNKS), CHUNKS) for s in steps]
        a, x, g = stepped((packed.at[0], packed.at[1], packed.at[2]), places)
        sums = [[None] * count for _ in steps]
        for n in range(STATE):
            b = [spread_at(spread, s, n) for s in steps]
            c = [spread_at(spread, s, STATE + n) for s in steps]
            terms = [None] * AT_ONCE
            for t in range(count):
                held = later[t, state_at(n), :]
                for k in range(AT_ONCE - 1, -1, -1):
                    adj = held + g[k][t] * c[k]
                    term = adj * b[k]
                    sums[k][t] = term if n == 0 else sums[k][t] + term
                    term = adj * x[k][t]
                    terms[k] = term if t == 0 else terms[k] + term
                    held = a[k][t] * adj
                later[t, state_at(n), :] = held
            keep_products(i, n, terms)
        for t in range(count):
            total = log_sum[t]
            for k in range(AT_ONCE - 1, -1, -1):
                target = pl.ds(steps[k], CHUNKS, stride=length)
                dx = sums[k][t]
                total = total + packed[3, t, places[k], :] - x[k][t] * dx
                total = jnp.where(a[k][t] == 0.0, 0.0, total)
                gx[t, target, :] = dx
                glog[t, target, :] = total
            log_sum[t] = total
        return carry

    lax.fori_loop(0, length // AT_ONCE, backward, 0)
    mixed[...] += jnp.dot(products[...], pick_b_ref[...], preferred_element_type=F32)

    @pl.when(pl.program_id(0) == pl.num_programs(0) - 1)
    def _():
        for j in range(CHUNKS):
            gbc_ref[j * length : (j + 1) * length, :] = mixed[
                pl.ds(j, length, stride=CHUNKS), :
            ].astype(BF16)

    rate = -jnp.exp(par_ref[0:1, :])
    skip = par_ref[2:3, :]
    u = u_ref[...]
    raw = pre_ref[...] + par_ref[1:2, :]
    step = softplus(raw)
    dx = get(gx, slice(None))
    dlog = get(glog, slice(None))
    gpre = (dlog * rate + dx * u) * sigmoid(raw)
    sig = sigmoid(gate)
    gu_ref[...] = (g * skip + dx * step).astype(BF16)
    gz_ref[...] = (
        grad_ref[...] * (scanned_ref[...] + skip * u) * (sig * (1.0 + gate * (1.0 - sig)))
    ).astype(BF16)
    gp_ref[...] = gpre.astype(BF16)
    gpar_ref[0:1, :] = jnp.sum(dlog * step, axis=0, keepdims=True) * rate
    gpar_ref[1:2, :] = jnp.sum(gpre, axis=0, keepdims=True)
    gpar_ref[2:3, :] = jnp.sum(g * u, axis=0, keepdims=True)
    gpar_ref[3:8, :] = jnp.zeros((5, count * LANES), F32)


class ScanCalls:
    def __init__(self, rows, wide, me):
        self.rows, self.wide, self.me = rows, wide, me
        self.length = rows // CHUNKS
        tiles = wide // LANES
        self.count = 2 if tiles % 2 == 0 else 1
        self.lanes = self.count * LANES
        self.steps = tiles // self.count
        self.bc_spec = pl.BlockSpec((rows, LANES), lambda t: (0, 3 * tiles))
        self.keep_spec = pl.BlockSpec((rows, LANES), lambda t: (0, 0))
        self.tile = pltpu.VMEM((self.count, rows, LANES), F32)
        self.thin = pltpu.VMEM((rows, LANES), F32)
        self.spread = pltpu.VMEM((rows, 2 * STATE * LANES), F32)
        self.packed = STATE * CHUNKS
        self.states = pltpu.VMEM((self.count, self.packed, LANES), F32)

    def tall(self, part):
        steps = self.steps
        return pl.BlockSpec((self.rows, self.lanes), lambda t: (0, part * steps + t))

    def flat(self, height):
        return pl.BlockSpec((height, self.lanes), lambda t: (0, t))

    def out(self, height, kind=F32):
        return jax.ShapeDtypeStruct((height, self.wide), kind)

    def call(self, kernel, in_specs, out_specs, out_shape, scratch, flops, moved):
        return pl.pallas_call(
            functools.partial(kernel, self.length, self.count),
            grid=(self.steps,),
            in_specs=[pl.BlockSpec(memory_space=pltpu.SMEM)] + in_specs,
            out_specs=out_specs,
            out_shape=out_shape,
            scratch_shapes=scratch,
            compiler_params=kernel_params(),
            cost_estimate=cost(flops, moved),
        )

    def before(self, proj, keep, par):
        return self.call(
            before_kernel,
            [self.tall(0), self.tall(2), self.bc_spec, self.keep_spec, self.flat(8)],
            [self.flat(self.packed), self.flat(CHUNKS), self.flat(STATE + 8)],
            [self.out(self.packed), self.out(CHUNKS), self.out(STATE + 8)],
            [self.tile, self.tile, self.states],
            2e9,
            self.rows * self.wide * 8,
        )(self.me, proj, proj, proj, keep, par)

    def scan(self, proj, keep, par, ends, tail, carried):
        return self.call(
            scan_kernel,
            [self.tall(0), self.tall(1), self.tall(2), self.bc_spec, self.keep_spec, self.flat(8)]
            + [self.flat(self.packed), self.flat(CHUNKS), self.flat(STATE)],
            [self.tall(0), self.tall(0), self.flat(self.packed)],
            [self.out(self.rows, BF16), self.out(self.rows), self.out(self.packed)],
            [self.spread, self.thin, self.tile, self.tile, self.tile, self.states, self.states],
            8e9,
            self.rows * self.wide * 18,
        )(self.me, proj, proj, proj, proj, keep, par, ends, tail, carried)

    def after(self, grad_mid, proj, keep, par, tail):
        return self.call(
            after_kernel,
            [self.tall(0), self.tall(1), self.tall(2), self.bc_spec, self.keep_spec, self.flat(8)]
            + [self.flat(CHUNKS)],
            [self.flat(self.packed), self.flat(STATE)],
            [self.out(self.packed), self.out(STATE)],
            [self.tile, self.tile, self.states],
            2e9,
            self.rows * self.wide * 12,
        )(self.me, grad_mid, proj, proj, proj, keep, par, tail)

    def back(self, grad_mid, proj, keep, par, tail, scanned, start, heads, carried):
        lane = jnp.arange(STATE * LANES, dtype=jnp.int32)[:, None] // LANES
        column = jnp.arange(LANES, dtype=jnp.int32)[None, :]
        pick_b = (lane == column).astype(BF16)
        pick_c = (lane + STATE == column).astype(BF16)
        pick_spec = pl.BlockSpec((STATE * LANES, LANES), lambda t: (0, 0))
        products = pltpu.VMEM((self.rows, STATE * LANES), BF16)
        return self.call(
            scan_back_kernel,
            [self.tall(0), self.tall(0), self.tall(1), self.tall(2), self.bc_spec]
            + [self.keep_spec, self.flat(8), self.flat(CHUNKS), self.tall(0)]
            + [self.flat(self.packed), self.flat(self.packed), self.flat(STATE)]
            + [pick_spec, pick_spec],
            [self.tall(0), self.tall(0), self.tall(0), self.keep_spec, self.flat(8)],
            [self.out(self.rows, BF16)] * 3
            + [jax.ShapeDtypeStruct((self.rows, LANES), BF16), self.out(8)],
            [self.spread, products] + [self.tile] * 5
            + [pltpu.VMEM((4, self.count, self.rows, LANES), F32)]
            + [self.states] * 3 + [self.thin, pltpu.VMEM((self.count, CHUNKS, LANES), F32)],
            4e10,
            self.rows * self.wide * 30,
        )(self.me, grad_mid, proj, proj, proj, proj, keep, par, tail, scanned, start, heads, carried, pick_b, pick_c)


def scores_of(base, q, keys, low_ref):
    scores = lax.dot_general(q, keys, (((1,), (1,)), ((), ())), preferred_element_type=F32)
    place = lax.broadcasted_iota(jnp.int32, scores.shape, 1) + base
    own = lax.broadcasted_iota(jnp.int32, scores.shape, 0) + (base + WINDOW)
    return jnp.where((place >= low_ref[...]) & (place <= own), scores, -1e30)


def turn_slots(value):
    return jnp.concatenate(
        [pltpu.roll(value[:, wide_lanes(t)], HEAD, 1) for t in range(2)], axis=1
    )


def lay_out(me_ref, block, parts, kv):
    for k, part in enumerate(parts):
        for j in range(CHUNKS):
            source = pl.multiple_of((me_ref[0] ^ j) * block, block)
            target = slice((k * CHUNKS + j) * block, (k * CHUNKS + j + 1) * block)
            value = part[pl.ds(source, block), :]
            kv[0, target, :] = value
            kv[1, target, :] = turn_slots(value.astype(F32)).astype(BF16)


def half_of(lane, h):
    return (lane < HEAD) if h % 2 == 0 else (lane >= HEAD)


def attend_kernel(heads, hops, me_ref, q_ref, *refs):
    parts, (low_ref, out_ref, log_ref, kv) = refs[: hops + 1], refs[hops + 1 :]
    block = q_ref.shape[0]

    @pl.when(pl.program_id(0) == 0)
    def _():
        lay_out(me_ref, block, parts, kv)

    base = (pl.program_id(0) ^ me_ref[0]) * block + (hops * CHUNKS * block - WINDOW)
    window = pl.ds(pl.multiple_of(base, LANES), WINDOW + block)
    lane = lax.broadcasted_iota(jnp.int32, (block, LANES), 1)
    logs = jnp.zeros((block, LANES), F32)
    mixes = []
    for h in range(heads):
        part = wide_lanes(h // 2)
        turned = me_ref[1 + h]
        q = jnp.where(half_of(lane, h), q_ref[:, part].astype(F32) * 0.125, 0.0).astype(BF16)
        scores = scores_of(base, q, kv[turned, window, :LANES], low_ref)
        top = jnp.max(scores, axis=1, keepdims=True)
        soft = jnp.exp(scores - top)
        total = jnp.sum(soft, axis=1, keepdims=True)
        mix = jnp.dot(soft.astype(BF16), kv[turned, window, LANES:], preferred_element_type=F32)
        mixes.append(mix * (1.0 / total))
        logs = jnp.where(lane == h, top + jnp.log(total), logs)
        if h % 2:
            out_ref[:, part] = jnp.where(lane < HEAD, mixes[h - 1], mixes[h]).astype(BF16)
    log_ref[...] = logs


def attend_back_kernel(heads, hops, me_ref, q_ref, *refs):
    parts, refs = refs[: hops + 1], refs[hops + 1 :]
    low_ref, log_ref, grad_ref, gq_ref = refs[:4]
    gparts, (kv, gkv) = refs[4 : hops + 5], refs[hops + 5 :]
    block = q_ref.shape[0]

    @pl.when(pl.program_id(0) == 0)
    def _():
        lay_out(me_ref, block, parts, kv)
        gkv[...] = jnp.zeros_like(gkv)

    base = (pl.program_id(0) ^ me_ref[0]) * block + (hops * CHUNKS * block - WINDOW)
    window = pl.ds(pl.multiple_of(base, LANES), WINDOW + block)
    lane = lax.broadcasted_iota(jnp.int32, (block, LANES), 1)
    across = (((0,), (0,)), ((), ()))
    gqs = []
    for h in range(heads):
        part = wide_lanes(h // 2)
        turned = me_ref[1 + h]
        keys = kv[turned, window, :LANES]
        mine = half_of(lane, h)
        q = jnp.where(mine, q_ref[:, part].astype(F32) * 0.125, 0.0).astype(BF16)
        grad = jnp.where(mine, grad_ref[:, part].astype(F32), 0.0).astype(BF16)
        soft = jnp.exp(scores_of(base, q, keys, low_ref) - log_ref[:, h : h + 1])
        gsoft = lax.dot_general(
            grad, kv[turned, window, LANES:], (((1,), (1,)), ((), ())), preferred_element_type=F32
        )
        delta = jnp.sum(soft * gsoft, axis=1, keepdims=True)
        gscore = (soft * (gsoft - delta)).astype(BF16)
        gqs.append(jnp.dot(gscore, keys, preferred_element_type=F32) * 0.125)
        gkv[turned, window, :LANES] += lax.dot_general(
            gscore, q, across, preferred_element_type=F32
        )
        gkv[turned, window, LANES:] += lax.dot_general(
            soft.astype(BF16), grad, across, preferred_element_type=F32
        )
        if h % 2:
            gq_ref[:, part] = jnp.where(lane < HEAD, gqs[h - 1], gqs[h]).astype(BF16)

    @pl.when(pl.program_id(0) == pl.num_programs(0) - 1)
    def _():
        for k, part in enumerate(gparts):
            for j in range(CHUNKS):
                target = pl.multiple_of((me_ref[0] ^ j) * block, block)
                source = slice((k * CHUNKS + j) * block, (k * CHUNKS + j + 1) * block)
                part[pl.ds(target, block), :] = (
                    gkv[0, source, :] + turn_slots(gkv[1, source, :])
                ).astype(part.dtype)


def attend_specs(rows, hops):
    block = rows // CHUNKS
    by_row = lambda width: pl.BlockSpec((block, width), lambda b: (b, 0))
    whole = [pl.BlockSpec((rows, 2 * LANES), lambda b: (0, 0))] * (hops + 1)
    total = (hops + 1) * rows
    return by_row, whole, total, pl.BlockSpec(memory_space=pltpu.SMEM)


def attend(heads, me, q, kvs, low):
    rows, wide = q.shape
    by_row, whole, total, scalar = attend_specs(rows, len(kvs) - 1)
    return pl.pallas_call(
        functools.partial(attend_kernel, heads, len(kvs) - 1),
        grid=(CHUNKS,),
        in_specs=[scalar, by_row(wide), *whole, by_row(1)],
        out_specs=[by_row(wide), by_row(LANES)],
        out_shape=[
            jax.ShapeDtypeStruct((rows, wide), BF16),
            jax.ShapeDtypeStruct((rows, LANES), F32),
        ],
        scratch_shapes=[pltpu.VMEM((2, total, 2 * LANES), BF16)],
        compiler_params=kernel_params(),
        cost_estimate=cost(6e9, 8e6),
    )(me, q, *kvs, low)


def attend_back(heads, me, q, kvs, low, logs, grad):
    rows, wide = q.shape
    by_row, whole, total, scalar = attend_specs(rows, len(kvs) - 1)
    part = jax.ShapeDtypeStruct((rows, 2 * LANES), BF16)
    own = jax.ShapeDtypeStruct((rows, 2 * LANES), F32)
    return pl.pallas_call(
        functools.partial(attend_back_kernel, heads, len(kvs) - 1),
        grid=(CHUNKS,),
        in_specs=[scalar, by_row(wide), *whole, by_row(1), by_row(LANES), by_row(wide)],
        out_specs=[by_row(wide), *whole],
        out_shape=[jax.ShapeDtypeStruct((rows, wide), BF16)] + [part] * (len(kvs) - 1) + [own],
        scratch_shapes=[
            pltpu.VMEM((2, total, 2 * LANES), BF16),
            pltpu.VMEM((2, total, 2 * LANES), F32),
        ],
        compiler_params=kernel_params(),
        cost_estimate=cost(3e10, 1.2e7),
    )(me, q, *kvs, low, logs, grad)


def swap_cores(value):
    return lax.ppermute(value, "core", [(0, 1), (1, 0)])


def from_peer(value, k):
    return lax.ppermute(value, "tp", [(n, n ^ k) for n in range(lax.axis_size("tp"))])


def team_gather(rows):
    tps = lax.axis_size("tp")
    got = {k: from_peer(rows, k) for k in range(tps - 1, 0, -1)}
    own = jnp.concatenate([rows] + [got[k] for k in range(1, tps)], axis=0)
    return jnp.concatenate([own, swap_cores(own)], axis=0)


def team_pair(values):
    half = values.shape[0] // CORES
    block = half // lax.axis_size("tp")
    other = swap_cores(values[half:])
    low = (values[:half].astype(F32) + other.astype(F32)).astype(BF16)
    return low, values[:block].astype(F32) + other[:block].astype(F32)


def peers_sum(low, total):
    tps = lax.axis_size("tp")
    block = low.shape[0] // tps
    for part in [from_peer(low[k * block : (k + 1) * block], k) for k in range(tps - 1, 0, -1)]:
        total = total + part.astype(F32)
    return total


def team_scatter(values):
    low, total = team_pair(values)
    return peers_sum(low, total), low


def peer_reduce(value):
    tps, own = lax.axis_size("tp"), lax.axis_index("tp")
    block = round_up(value.shape[1], tps * LANES) // tps
    value = jnp.pad(value, ((0, 0), (0, tps * block - value.shape[1])))
    parts = [lax.dynamic_slice_in_dim(value, (own ^ k) * block, block, 1) for k in range(tps)]
    total = parts[0]
    for k in range(1, tps):
        total = total + from_peer(parts[k].astype(BF16), k).astype(F32)
    return total.astype(BF16)


def peer_spread(part):
    tps, own = lax.axis_size("tp"), lax.axis_index("tp")
    block = part.shape[1]
    whole = jnp.zeros((part.shape[0], tps * block), BF16)
    for k in range(tps):
        got = from_peer(part, k) if k else part
        whole = lax.dynamic_update_slice_in_dim(whole, got, (own ^ k) * block, 1)
    return whole


def shifted(value, steps):
    count = lax.axis_size("chip")
    leading, last = (max(0, -steps), min(count, count - steps))
    return lax.ppermute(value, "chip", [(k, k + steps) for k in range(leading, last)])


def behind(value, *others):
    if len(others) > 1:
        value = behind(value, *others[:-1])
    other = others[-1]
    last = other[(slice(-1, None),) * other.ndim].reshape((1,) * value.ndim)
    return value + (last * 0).astype(value.dtype)


def chip_gather(value):
    chips = lax.axis_size("chip")
    if chips != 4:
        return lax.all_gather(value, "chip")
    own = lax.axis_index("chip")
    got = jnp.stack(
        [value] + [lax.ppermute(value, "chip", [(n, n ^ k) for n in range(chips)]) for k in range(1, chips)]
    )
    return jnp.concatenate([lax.dynamic_slice_in_dim(got, own ^ k, 1, 0) for k in range(chips)])


def by_core(mine, other):
    first = lax.axis_index("core") == 0
    return jnp.where(first, mine, other), jnp.where(first, other, mine)


def to_rows(values):
    tps = lax.axis_size("tp")
    half = values.shape[0] // CORES
    block = half // tps
    wide = CORES * values.shape[1]
    pair = jnp.concatenate(by_core(values[:half], swap_cores(values[half:])), axis=1)
    got = [pair[:block]] + [from_peer(pair[k * block : (k + 1) * block], k) for k in range(1, tps)]
    whole = jnp.zeros((block, tps * wide), values.dtype)
    for k in range(tps):
        place = (lax.axis_index("tp") ^ k) * wide
        whole = lax.dynamic_update_slice_in_dim(whole, got[k], place, 1)
    return whole


def to_columns(values):
    tps = lax.axis_size("tp")
    wide = values.shape[1] // tps
    parts = [
        lax.dynamic_slice_in_dim(values, (lax.axis_index("tp") ^ k) * wide, wide, 1)
        for k in range(tps)
    ]
    pair = jnp.concatenate([parts[0]] + [from_peer(parts[k], k) for k in range(1, tps)], axis=0)
    mine, other = by_core(pair[:, : wide // CORES], pair[:, wide // CORES :])
    return jnp.concatenate([mine, swap_cores(other)], axis=0)


def core_pair(shard, rows):
    core = lax.axis_index("core")
    mine = lax.dynamic_index_in_dim(shard, core, 1, False)
    other = swap_cores(lax.dynamic_index_in_dim(shard, 1 - core, 1, False))
    pair = jnp.concatenate(by_core(mine, other), axis=0)
    return jnp.pad(pair, ((0, rows - pair.shape[0]), (0, 0)))


def summed_rows(full):
    return behind(lax.psum_scatter(full, "chip", scatter_dimension=0, tiled=True), full)


def split_cores(rows, count):
    rows = rows[: CORES * count].reshape(CORES, count, -1)
    core = lax.axis_index("core")
    mine = lax.dynamic_index_in_dim(rows, core, 0, False)
    return mine, swap_cores(lax.dynamic_index_in_dim(rows, 1 - core, 0, False))


def share_columns(pair):
    tps = lax.axis_size("tp")
    whole = jnp.concatenate([pair] + [from_peer(pair, k) for k in range(1, tps)], axis=0)
    own = lax.axis_index("tp") * CORES + lax.axis_index("core")
    return jnp.concatenate(
        [lax.dynamic_slice_in_dim(whole, own ^ k, 1, 0) for k in range(CORES * tps)], axis=0
    )


def body(
    x_in, lengths, w_q, w_kv, w_o, input_weight, a_log, dt_bias, d_skip,
    w_bc, w_out, gains, gate_up_weight, w_down, cotangent,
):
    chips, tps = lax.axis_size("chip"), lax.axis_size("tp")
    chip, core, tp = (lax.axis_index(name) for name in ("chip", "core", "tp"))
    team = CORES * tps
    unit = tp * CORES + core
    layers, shard_rows, width = w_q.shape
    rows_own, features = x_in.shape
    part = features // chips
    part_wide = round_up(features, LANES) // chips
    padded = part_wide * chips
    rows = rows_own * team
    hops = -(-WINDOW // rows)
    kv_half = w_kv.shape[2] // 2
    heads_here = -(-HEADS // team)
    q_wide = heads_here * HEAD
    slot_wide = SLOTS * HEAD
    channels = a_log.shape[1] // CORES
    wide = round_up(channels, LANES)
    hidden_here = gate_up_weight.shape[3] // CORES
    hidden_wide = round_up(hidden_here, LANES)
    me = (core * tps + tp).astype(jnp.int32)
    me_array = jnp.reshape(me, (1,))
    scan = ScanCalls(rows, wide, me_array)
    sums = [None] * layers

    order = jnp.arange(team, dtype=jnp.int32) ^ me
    local = order[:, None] * rows_own + jnp.arange(rows_own, dtype=jnp.int32)[None, :]
    places = chip * rows + local.reshape(rows)
    starts = (jnp.cumsum(lengths) - lengths).astype(jnp.int32)
    reached = places[:, None] >= starts[None, :]
    opening = jnp.any(places[:, None] == starts[None, :], axis=1)
    keep = jnp.broadcast_to((1.0 - opening.astype(F32))[:, None], (rows, LANES))
    first = jnp.max(jnp.where(reached, starts[None, :], 0), axis=1)
    low = jnp.maximum(first, places - (WINDOW - 1)) - (chip - hops) * rows
    low = low[:, None]

    head_ids = unit * heads_here + jnp.arange(heads_here, dtype=jnp.int32)
    slot_ids = head_ids // GROUP - (unit * heads_here) // GROUP
    turns = (slot_ids ^ jnp.arange(heads_here, dtype=jnp.int32)) & 1
    attend_array = jnp.concatenate([me_array, turns.astype(jnp.int32)])

    def spaced(values):
        values = values.reshape(values.shape[:-1] + (chips, part))
        return pad_lanes(values, part_wide).reshape(values.shape[:-2] + (padded,))

    def unspaced(values):
        values = values.reshape(values.shape[:-1] + (chips, part_wide))[..., :part]
        return values.reshape(values.shape[:-2] + (features,))

    def pad_lanes(values, size):
        return jnp.pad(values, [(0, 0)] * (values.ndim - 1) + [(0, size - values.shape[-1])])

    def kv_columns(layer, index):
        base = (index * heads_here) // GROUP * HEAD
        whole = jnp.pad(w_kv[layer].reshape(shard_rows, 2, kv_half), ((0, 0), (0, 0), (0, slot_wide)))
        return lax.dynamic_slice_in_dim(whole, base, slot_wide, 2).reshape(shard_rows, 2 * slot_wide)

    place = chip * CORES + core

    def prepare_mixer_in(layer):
        ins = input_weight[layer].reshape(shard_rows, 3, CORES, channels)
        ins = pad_lanes(ins.transpose(0, 2, 1, 3), wide).reshape(shard_rows, CORES, 3 * wide)
        bcs = lax.dynamic_slice_in_dim(w_bc[layer], place * shard_rows, shard_rows, 0)
        bcs = jnp.broadcast_to(pad_lanes(bcs, LANES)[:, None], (shard_rows, CORES, LANES))
        qs = lax.dynamic_slice_in_dim(
            pad_lanes(w_q[layer], team * q_wide), tp * CORES * q_wide, CORES * q_wide, 1
        ).reshape(shard_rows, CORES, q_wide)
        kvs = jnp.stack([kv_columns(layer, tp * CORES + k) for k in range(CORES)], axis=1)
        return core_pair(jnp.concatenate([ins, bcs, qs, kvs], axis=2), part_wide)

    def prepare_mixer_out(layer):
        return core_pair(
            pad_lanes(w_out[layer].T.reshape(shard_rows, CORES, channels), wide), part_wide
        )

    def prepare_ffn(layer):
        gus = gate_up_weight[layer].reshape(shard_rows, 2, CORES, hidden_here)
        gus = pad_lanes(gus.transpose(0, 2, 1, 3), hidden_wide)
        gus = gus.reshape(shard_rows, CORES, 2 * hidden_wide)
        downs = pad_lanes(w_down[layer].T.reshape(shard_rows, CORES, hidden_here), hidden_wide)
        return core_pair(jnp.concatenate([gus, downs], axis=2), part_wide)

    def of_chips(pair):
        return lax.all_gather(pair, "chip", axis=0, tiled=True)

    def scan_params(layer):
        mine = [
            lax.dynamic_slice_in_dim(part[layer], core * channels, channels, 0)
            for part in (a_log, dt_bias, d_skip)
        ]
        return jnp.pad(jnp.stack(mine), ((0, 5), (0, wide - channels)))

    def chain(everything, back):
        state = jnp.zeros(everything[0][0].shape, F32)
        order = range(chips - 1, -1, -1) if back else range(chips)
        for k in order:
            counts = (k > chip) if back else (k < chip)
            new = everything[1][k][None, :] * state + everything[0][k]
            state = jnp.where(counts, new, state)
        return state

    norm = functools.partial(rms_scale, features)
    mix = functools.partial(branch_mix, features)

    def norm_in(stream, layer):
        return team_gather(norm(stream, gains[layer, 0]).astype(BF16))

    def forward_layer(stream, normed_all, layer, weights, aside=None):
        w_in, w_ssm, w_attn, w_mamba, w_attn_out, w_gu, w_dn = weights
        gain = gains[layer]
        par = scan_params(layer)
        qkv = dot(normed_all, w_attn, BF16)
        kv = qkv[:, q_wide:]
        others = [team_gather(behind(aside, kv))] if aside is not None else []
        kvs = [shifted(kv, hop) for hop in range(hops, 0, -1)] + [kv]
        proj = behind(dot(normed_all, w_ssm), kv)
        ends, tail, dev = scan.before(proj, keep, par)
        devs = chip_gather(behind(dev, kvs[0]))
        chip_decay = devs[:, STATE]
        carried = chain((devs[:, :STATE], chip_decay), False)
        q = qkv[:, :q_wide]
        attended, logs = attend(heads_here, attend_array, q, kvs, behind(low, dev))
        own_attended = to_rows(attended)[:, :width]
        mid, scanned, start = scan.scan(
            proj, keep, behind(par, attended, *others), ends, tail, carried
        )
        mamba_out, low_out = team_scatter(dot_nt(behind(mid, own_attended), w_mamba, BF16))
        attn_out = dot(behind(own_attended, low_out), w_attn_out)
        middle = stream + mix(attn_out, mamba_out, gain[1], gain[2])
        ffn_all = team_gather(norm(middle, gain[3]).astype(BF16))
        gate_up = dot(ffn_all, w_gu)
        hidden = swiglu(gate_up).astype(BF16)
        ffn_part = dot_nt(hidden, w_dn, BF16)
        kept = dict(
            stream=stream, normed_all=normed_all, q=q, kvs=kvs, logs=logs,
            own_attended=own_attended, proj=proj, tail=tail, chip_decay=chip_decay, mid=mid,
            scanned=scanned, start=start, attn_out=attn_out, mamba_out=mamba_out, middle=middle,
            ffn_all=ffn_all, gate_up=gate_up, hidden=hidden, par=par,
        )
        return middle, ffn_part, kept, others

    def backward_layer(grad_out, grad_all, layer, weights, kept, aside):
        early = layer == 0
        w_in, w_ssm, w_attn, w_mamba, w_attn_out, w_gu, w_dn = weights
        gain = gains[layer]
        normed_all = kept["normed_all"]
        grad_hidden = dot(grad_all, w_dn)
        _, swiglu_pull = jax.vjp(swiglu, kept["gate_up"])
        grad_gu = swiglu_pull(grad_hidden)[0].astype(BF16)
        partial = dot_nt(grad_gu, w_gu, BF16)
        grad_ffn, low_ffn = team_scatter(partial)
        full_ffn = jnp.concatenate(
            [
                dot_tn(kept["ffn_all"], behind(grad_gu, low_ffn), BF16),
                dot_tn(grad_all, behind(kept["hidden"], low_ffn), BF16),
            ],
            axis=1,
        )
        ffn_sums = summed_rows(full_ffn)
        grad_ffn = behind(grad_ffn, full_ffn)
        _, norm_pull = jax.vjp(norm, kept["middle"], gain[3])
        grad_mid_norm, grad_gain_ffn = norm_pull(grad_ffn)
        grad_middle = grad_out + grad_mid_norm
        _, mix_pull = jax.vjp(mix, kept["attn_out"], kept["mamba_out"], gain[1], gain[2])
        grad_attn, grad_mamba, grad_gain_attn, grad_gain_mamba = mix_pull(grad_middle)
        grad_mamba_all = team_gather(grad_mamba.astype(BF16))
        grad_attn = grad_attn.astype(BF16)
        grad_att = pad_lanes(dot_nt(grad_attn, w_attn_out, BF16), team * q_wide)
        grad_att = to_columns(grad_att)
        full_o = dot_tn(spaced(kept["own_attended"]), behind(grad_attn, grad_att), BF16)
        gq, *gkvs = attend_back(
            heads_here, attend_array, kept["q"], kept["kvs"], low, kept["logs"], grad_att
        )
        gkv = gkvs[hops]
        for hop in range(1, hops + 1):
            gkv = gkv + shifted(gkvs[hops - hop], -hop).astype(F32)
        grad_qkv = jnp.concatenate([gq, gkv.astype(BF16)], axis=1)
        grad_mid = dot(grad_mamba_all, w_mamba)
        par = kept["par"]
        heads, dev = scan.after(grad_mid, kept["proj"], keep, behind(par, gq), kept["tail"])
        devs = chip_gather(dev)
        carried = chain((devs, kept["chip_decay"]), True)
        full_out = dot_tn(grad_mamba_all, behind(kept["mid"], dev), BF16)
        if early:
            full_qkv = dot_tn(normed_all, behind(grad_qkv, dev), BF16)
            full_mix = jnp.concatenate([full_qkv, full_out, full_o], axis=1)
            mix_sums = summed_rows(full_mix)
            par = behind(par, full_mix)
        else:
            par = behind(par, full_out, full_o, ffn_sums)
        gates, sides = aside()
        par = behind(par, *gates)
        gu, gz, gp, gbc, gpar = scan.back(
            grad_mid, kept["proj"], keep, par, kept["tail"], kept["scanned"], kept["start"], heads, carried
        )
        gbc = behind(gbc, *sides)
        grad_proj = jnp.concatenate([gu, gz, gp, gbc, grad_qkv], axis=1)
        if early:
            full_in = dot_tn(normed_all, grad_proj[:, : 3 * wide + LANES], BF16)
            ssm_sums = summed_rows(full_in)
            partial = dot_nt(behind(grad_proj, full_in), w_in, BF16)
            grad_normed, low_normed = team_scatter(partial)
        else:
            partial = dot_nt(grad_proj, w_in, BF16)
            grad_normed, low_normed = team_scatter(partial)
            full_in = dot_tn(normed_all, behind(grad_proj, low_normed), BF16)
            grad_normed = behind(grad_normed, full_in)
            mix_sums = summed_rows(jnp.concatenate([full_in, full_out, full_o], axis=1))
            ssm_sums = mix_sums[:, : 3 * wide + LANES]
            mix_sums = mix_sums[:, 3 * wide + LANES :]
        _, in_pull = jax.vjp(norm, kept["stream"], gain[0])
        grad_stream_norm, grad_gain_in = in_pull(grad_normed)
        grad_gains = jnp.stack([grad_gain_in, grad_gain_attn, grad_gain_mamba, grad_gain_ffn])
        small = jnp.concatenate([grad_gains.reshape(-1), gpar[:3, :channels].reshape(-1)])
        later = dict(ffn=ffn_sums, ssm=ssm_sums, mix=mix_sums, small=small)
        return grad_middle + grad_stream_norm, later

    gains = spaced(gains)
    stream = spaced(x_in).astype(F32)
    cotangent = spaced(cotangent)
    normed_all = norm_in(stream, 0)
    pairs = [(prepare_mixer_in(l), prepare_mixer_out(l), prepare_ffn(l)) for l in range(layers)]
    weights = []
    for layer in range(layers):
        ins, outs, ffn = pairs[layer]
        if layer == 0:
            ins = of_chips(ins)
            lead = normed_all
        else:
            ins = of_chips(behind(ins, lead))
        outs = of_chips(behind(outs, lead))
        o = lax.all_gather(behind(spaced(w_o[layer]), lead), ("chip", "core"), axis=0, tiled=True)
        ffn = of_chips(behind(ffn, lead))
        first = 3 * wide + LANES
        weights.append(
            (
                ins, ins[:, :first], ins[:, first:], outs, o,
                ffn[:, : 2 * hidden_wide], ffn[:, 2 * hidden_wide :],
            )
        )
    kept = []
    for layer in range(layers):
        if layer:
            normed_all = norm_in(stream, layer)
        middle, ffn_part, saved, others = forward_layer(
            stream, normed_all, layer, weights[layer], None if layer else cotangent
        )
        if layer == 0:
            grad_all = others[0]
        kept.append(saved)
        if layer + 1 < layers:
            stream = middle + team_scatter(ffn_part)[0]
    grad_stream = cotangent.astype(F32)
    shares = [None] * layers
    grad_os = [None] * layers
    out_sums = [None] * layers

    qkv_wide = q_wide + 2 * slot_wide

    def mix_parts(layer):
        mine, other = split_cores(sums[layer]["mix"], shard_rows)
        ours = mine[:, qkv_wide + wide :].astype(F32) + other[:, qkv_wide + wide :].astype(F32)
        out_sums[layer] = (mine[:, qkv_wide : qkv_wide + wide], other[:, qkv_wide : qkv_wide + wide])
        return jnp.stack([mine[:, :qkv_wide], other[:, :qkv_wide]]), ours

    for layer in range(layers - 1, -1, -1):
        if layer + 1 < layers:
            grad_all = team_gather(grad_stream.astype(BF16))
        found = []

        def aside(layer=layer, found=found):
            if layer + 1 == layers:
                low_out, total = team_pair(ffn_part)
                found.append(peers_sum(low_out, total))
                return (low_out,), found
            pair, ours = mix_parts(layer + 1)
            shares[layer + 1] = share_columns(pair)
            grad_os[layer + 1] = peer_spread(peer_reduce(ours))
            return (pair, ours), (shares[layer + 1], grad_os[layer + 1])

        grad_stream, sums[layer] = backward_layer(
            grad_stream, grad_all, layer, weights[layer], kept[layer], aside
        )
        if layer + 1 == layers:
            block_out = unspaced((middle + found[0]).astype(BF16))
    pair, ours = mix_parts(0)
    grad_os[0] = peer_spread(peer_reduce(ours))
    shares[0] = share_columns(pair)

    shared = jnp.stack(shares).transpose(0, 2, 1, 3)
    grad_o = unspaced(jnp.stack(grad_os)[..., :padded]).astype(F32)
    grad_q = shared[..., :q_wide].reshape(layers, shard_rows, team * q_wide)
    grad_q = grad_q[..., :width].astype(F32)
    kv_parts = shared[..., q_wide:].astype(F32)
    kv_parts = kv_parts.reshape(layers, shard_rows, team, 2, SLOTS, HEAD)
    kv_heads = []
    for head in range(KV_HEADS):
        terms = [
            kv_parts[:, :, k, :, slot]
            for k in range(team)
            for slot in range(SLOTS)
            if (k * heads_here) // GROUP + slot == head
        ]
        kv_heads.append(sum(terms[1:], terms[0]))
    grad_kv = jnp.stack(kv_heads, axis=3).reshape(layers, shard_rows, 2 * kv_half)
    ssm_sums = [split_cores(parts["ssm"], shard_rows) for parts in sums]
    ffn_sums = [split_cores(parts["ffn"], shard_rows) for parts in sums]

    def halves(sums_of, begin, end):
        return [
            jnp.stack(by_core(*(part[:, begin:end] for part in parts))).astype(F32)
            for parts in sums_of
        ]

    grad_in = jnp.stack(
        [
            pair.reshape(CORES, shard_rows, 3, wide)[..., :channels]
            .transpose(1, 2, 0, 3)
            .reshape(shard_rows, 3, CORES * channels)
            for pair in halves(ssm_sums, 0, 3 * wide)
        ]
    )
    grad_out = jnp.stack(
        [
            pair.transpose(0, 2, 1).reshape(CORES * channels, shard_rows)
            for pair in halves(out_sums, 0, channels)
        ]
    )
    grad_gu = jnp.stack(
        [
            pair.reshape(CORES, shard_rows, 2, hidden_wide)[..., :hidden_here]
            .transpose(1, 2, 0, 3)
            .reshape(shard_rows, 2, CORES * hidden_here)
            for pair in halves(ffn_sums, 0, 2 * hidden_wide)
        ]
    )
    grad_down = jnp.stack(
        [
            pair.transpose(0, 2, 1).reshape(CORES * hidden_here, shard_rows)
            for pair in halves(ffn_sums, 2 * hidden_wide, 2 * hidden_wide + hidden_here)
        ]
    )
    small = jnp.sum(chip_gather(jnp.stack([parts["small"] for parts in sums])), axis=0)
    other = swap_cores(small)
    gain_part = small[:, : 4 * padded] + other[:, : 4 * padded]
    ssm_pair = jnp.concatenate(by_core(small[:, 4 * padded :], other[:, 4 * padded :]), axis=1)
    tiny = jnp.concatenate([gain_part, ssm_pair], axis=1)
    bc_part = jnp.concatenate(
        [mine[:, 3 * wide :].astype(F32) + theirs[:, 3 * wide :].astype(F32) for mine, theirs in ssm_sums]
    )
    tiny_got = [from_peer(tiny, k) for k in range(1, tps)]
    bc_got = [from_peer(bc_part.astype(BF16), k) for k in range(1, tps)]
    grad_bc = sum((got.astype(F32) for got in bc_got), bc_part)[:, : 2 * STATE]
    grad_bc = grad_bc.reshape(layers, shard_rows, 2 * STATE)
    gain_full = sum((got[:, : 4 * padded] for got in tiny_got), gain_part)
    gain_full = unspaced(gain_full.reshape(layers, 4, padded))
    ssm_all = jnp.stack([ssm_pair] + [got[:, 4 * padded :] for got in tiny_got])
    ssm_all = jnp.concatenate(
        [lax.dynamic_slice_in_dim(ssm_all, tp ^ k, 1, 0) for k in range(tps)]
    )
    ssm_full = ssm_all.reshape(tps, layers, CORES, 3, channels)
    ssm_full = ssm_full.transpose(1, 3, 0, 2, 4).reshape(layers, 3, team * channels)
    share = team * channels // (chips * CORES)
    ssm_own = lax.dynamic_slice_in_dim(ssm_full, place * share, share, 2)
    grad_gains = lax.dynamic_slice_in_dim(gain_full, place * shard_rows, shard_rows, 2)
    return (
        block_out, unspaced(grad_stream), grad_q, grad_kv, grad_o, grad_in,
        ssm_own[:, 0], ssm_own[:, 1], ssm_own[:, 2], grad_bc, grad_out, grad_gains, grad_gu, grad_down,
    )


def solution(mesh):
    fsdp, tp = mesh.shape["fsdp"], mesh.shape["tp"]
    inner = Mesh(mesh.devices.reshape(fsdp // CORES, CORES, tp), ("chip", "core", "tp"))
    shards = ("chip", "core")
    tokens = P(("chip", "core", "tp"), None)
    by_row = P(None, shards, None)
    return jax.shard_map(
        body,
        mesh=inner,
        in_specs=(
            tokens, P(), by_row, by_row, by_row, P(None, shards, None, "tp"),
            P(None, "tp"), P(None, "tp"), P(None, "tp"), P(), P(None, "tp", shards), P(),
            P(None, shards, None, "tp"), P(None, "tp", shards), tokens,
        ),
        out_specs=(
            tokens, tokens, by_row, by_row, by_row, P(None, shards, None, "tp"),
            P(None, shards), P(None, shards), P(None, shards), by_row, P(None, "tp", shards),
            P(None, None, shards), P(None, shards, None, "tp"), P(None, "tp", shards),
        ),
        check_vma=False,
    )
```

```python
import functools

import jax
import jax.numpy as jnp
from jax import lax
from jax.experimental import pallas as pl
from jax.experimental.pallas import tpu as pltpu
from jax.sharding import Mesh
from jax.sharding import PartitionSpec as P

HEADS = 25
HEAD = 64
KV_HEADS = 5
GROUP = HEADS // KV_HEADS
WINDOW = 1024
STATE = 16
EPSILON = 1e-05
TOP_PRECISION = lax.Precision.HIGHEST

CORES = 2
CHUNKS = 8
AT_ONCE = 4
LANES = 128
SLOTS = 2
VMEM_BYTES = 56 * 1024 * 1024
F32 = jnp.float32
BF16 = jnp.bfloat16


def round_up(value, unit):
    return -(-value // unit) * unit


def dot(a, b, out=F32):
    return jnp.dot(a, b, preferred_element_type=F32).astype(out)


def dot_nt(a, b, out=F32):
    return lax.dot_general(
        a, b, (((1,), (1,)), ((), ())), preferred_element_type=F32
    ).astype(out)


def dot_tn(a, b, out=F32):
    return lax.dot_general(
        a, b, (((0,), (0,)), ((), ())), preferred_element_type=F32
    ).astype(out)


def rms_scale(count, values, gain_row):
    mean = jnp.sum(values * values, axis=-1, keepdims=True) / count
    return values * lax.rsqrt(mean + EPSILON) * gain_row


def branch_mix(count, attn_out, mamba_out, gain_attn, gain_mamba):
    return 0.5 * (
        rms_scale(count, attn_out, gain_attn) + rms_scale(count, mamba_out, gain_mamba)
    )


def swiglu(gate_up_product):
    half = gate_up_product.shape[1] // 2
    return jax.nn.silu(gate_up_product[:, :half]) * gate_up_product[:, half:]


def softplus(v):
    return jnp.maximum(v, 0.0) + jnp.log1p(jnp.exp(-jnp.abs(v)))


def sigmoid(v):
    return 1.0 / (1.0 + jnp.exp(-v))


def kernel_params(bytes_limit=VMEM_BYTES):
    return pltpu.CompilerParams(
        dimension_semantics=("arbitrary",), vmem_limit_bytes=bytes_limit
    )


def cost(flops, moved):
    return pl.CostEstimate(flops=int(flops), bytes_accessed=int(moved), transcendentals=0)


def spread_bc(bc_ref, spread, turned, length):
    def turn(s, carry):
        place = pl.ds(pl.multiple_of(s * CHUNKS, CHUNKS), CHUNKS)
        turned[place, :] = bc_ref[pl.ds(s, CHUNKS, stride=length), :]
        return carry

    lax.fori_loop(0, length, turn, 0, unroll=8)
    block = 2 * LANES
    for q in range(2 * STATE * LANES // block):
        row = lax.broadcasted_iota(jnp.int32, (LANES, block), 0)
        column = lax.broadcasted_iota(jnp.int32, (LANES, block), 1) + q * block
        pick = (row == column // LANES).astype(F32).astype(BF16)
        for r in range(CHUNKS * length // block):
            part = slice(r * block, (r + 1) * block)
            spread[part, q * block : (q + 1) * block] = jnp.dot(
                turned[part, :].astype(BF16), pick, preferred_element_type=F32
            )


def spread_at(spread, s, n):
    place = pl.ds(pl.multiple_of(s * CHUNKS, CHUNKS), CHUNKS)
    return spread[place, n * LANES : (n + 1) * LANES]


def wide_lanes(t):
    return slice(t * LANES, (t + 1) * LANES)


def put(ref, value):
    for t in range(ref.shape[0]):
        ref[t] = value[:, wide_lanes(t)]


def get(ref, rows):
    return jnp.concatenate([ref[t, rows, :] for t in range(ref.shape[0])], axis=1)


def put_rows(ref, rows, value):
    for t in range(ref.shape[0]):
        ref[t, rows, :] = value[:, wide_lanes(t)]


def fill_decay(u_ref, pre_ref, keep_ref, par_ref, decay, inflow, count):
    step = softplus(pre_ref[...] + par_ref[1:2, :])
    keep = jnp.concatenate([keep_ref[...]] * count, axis=1)
    put(decay, jnp.exp(-step * jnp.exp(par_ref[0:1, :])) * keep)
    if u_ref is not None:
        put(inflow, step * u_ref[...])


def state_at(n):
    return slice(n * CHUNKS, (n + 1) * CHUNKS)


def stepped(refs, rows):
    return [[[ref[t, part, :] for t in range(ref.shape[0])] for part in rows] for ref in refs]


def before_kernel(length, count, me_ref, u_ref, pre_ref, bc_ref, keep_ref, par_ref, ends_ref, tail_ref, dev_ref, decay, inflow, ends):
    fill_decay(u_ref, pre_ref, keep_ref, par_ref, decay, inflow, count)

    def walk(k, rest):
        rows = pl.ds(length - 1 - k, CHUNKS, stride=length)
        for t in range(count):
            inflow[t, rows, :] = inflow[t, rows, :] * rest[t]
        return tuple(rest[t] * decay[t, rows, :] for t in range(count))

    ones = jnp.ones((CHUNKS, LANES), F32)
    rest = lax.fori_loop(0, length, walk, (ones,) * count, unroll=8)
    tail_ref[...] = jnp.concatenate(rest, axis=1)
    for r in range(CHUNKS):
        part = pl.ds(r * length, length)
        end = lax.dot_general(
            bc_ref[part, :].astype(BF16),
            get(inflow, part).astype(BF16),
            (((0,), (0,)), ((), ())),
            preferred_element_type=F32,
        )
        put_rows(ends, pl.ds(r, STATE, stride=CHUNKS), end[:STATE])
    ends_ref[...] = get(ends, slice(None))
    state = jnp.zeros((STATE, count * LANES), F32)
    total = jnp.ones((1, count * LANES), F32)
    for j in range(CHUNKS):
        r = me_ref[0] ^ j
        fade = tail_ref[pl.ds(r, 1), :]
        state = fade * state + get(ends, pl.ds(r, STATE, stride=CHUNKS))
        total = total * fade
    dev_ref[0:STATE, :] = state
    dev_ref[STATE : STATE + 8, :] = jnp.broadcast_to(total, (8, count * LANES))


def scan_kernel(
    length, count, me_ref, u_ref, gate_ref, pre_ref, bc_ref, keep_ref, par_ref, ends_ref, tail_ref, carried_ref,
    mid_ref, scanned_ref, start_ref, spread, turned, decay, inflow, scanned, ends, start,
):
    @pl.when(pl.program_id(0) == 0)
    def _():
        spread_bc(bc_ref, spread, turned, length)

    fill_decay(u_ref, pre_ref, keep_ref, par_ref, decay, inflow, count)
    put(ends, ends_ref[...])
    state = carried_ref[...]
    for j in range(CHUNKS):
        r = me_ref[0] ^ j
        rows = pl.ds(r, STATE, stride=CHUNKS)
        put_rows(start, rows, state)
        state = tail_ref[pl.ds(r, 1), :] * state + get(ends, rows)
    start_ref[...] = get(start, slice(None))

    def walk(i, carry):
        steps = [i * AT_ONCE + k for k in range(AT_ONCE)]
        rows = [pl.ds(s, CHUNKS, stride=length) for s in steps]
        a, x = stepped((decay, inflow), rows)
        sums = [[None] * count for _ in steps]
        for n in range(STATE):
            b = [spread_at(spread, s, n) for s in steps]
            c = [spread_at(spread, s, STATE + n) for s in steps]
            for t in range(count):
                h = start[t, state_at(n), :]
                for k in range(AT_ONCE):
                    h = a[k][t] * h + x[k][t] * b[k]
                    term = h * c[k]
                    sums[k][t] = term if n == 0 else sums[k][t] + term
                start[t, state_at(n), :] = h
        for k, part in enumerate(rows):
            for t in range(count):
                scanned[t, part, :] = sums[k][t]
        return carry

    lax.fori_loop(0, length // AT_ONCE, walk, 0)
    gate = gate_ref[...]
    y = get(scanned, slice(None))
    scanned_ref[...] = y
    mid_ref[...] = ((y + par_ref[2:3, :] * u_ref[...]) * (gate * sigmoid(gate))).astype(BF16)


def after_kernel(length, count, me_ref, grad_ref, gate_ref, pre_ref, bc_ref, keep_ref, par_ref, tail_ref, heads_ref, dev_ref, decay, flow, heads):
    fill_decay(None, pre_ref, keep_ref, par_ref, decay, None, count)
    gate = gate_ref[...]
    put(flow, grad_ref[...] * (gate * sigmoid(gate)))

    def walk(s, run):
        rows = pl.ds(s, CHUNKS, stride=length)
        new = []
        for t in range(count):
            new.append(run[t] * decay[t, rows, :])
            flow[t, rows, :] = flow[t, rows, :] * new[t]
        return tuple(new)

    lax.fori_loop(0, length, walk, (jnp.ones((CHUNKS, LANES), F32),) * count, unroll=8)
    for r in range(CHUNKS):
        part = pl.ds(r * length, length)
        head = lax.dot_general(
            bc_ref[part, :].astype(BF16),
            get(flow, part).astype(BF16),
            (((0,), (0,)), ((), ())),
            preferred_element_type=F32,
        )
        put_rows(heads, pl.ds(r, STATE, stride=CHUNKS), head[STATE : 2 * STATE])
    heads_ref[...] = get(heads, slice(None))
    state = jnp.zeros((STATE, count * LANES), F32)
    for j in range(CHUNKS - 1, -1, -1):
        r = me_ref[0] ^ j
        state = tail_ref[pl.ds(r, 1), :] * state + get(heads, pl.ds(r, STATE, stride=CHUNKS))
    dev_ref[...] = state


def scan_back_kernel(
    length, count, me_ref, grad_ref, u_ref, gate_ref, pre_ref, bc_ref, keep_ref, par_ref, tail_ref, scanned_ref, start_ref,
    heads_ref, carried_ref, pick_b_ref, pick_c_ref,
    gu_ref, gz_ref, gp_ref, gbc_ref, gpar_ref,
    spread, products, decay, inflow, flow, gx, glog, packed, later, heads, start, mixed, log_sum,
):
    @pl.when(pl.program_id(0) == 0)
    def _():
        spread_bc(bc_ref, spread, mixed, length)
        mixed[...] = jnp.zeros_like(mixed)

    fill_decay(u_ref, pre_ref, keep_ref, par_ref, decay, inflow, count)
    gate = gate_ref[...]
    g = grad_ref[...] * (gate * sigmoid(gate))
    put(flow, g)
    put(gx, g * scanned_ref[...])
    put(heads, heads_ref[...])
    put(start, start_ref[...])
    state = carried_ref[...]
    for j in range(CHUNKS - 1, -1, -1):
        r = me_ref[0] ^ j
        rows = pl.ds(r, STATE, stride=CHUNKS)
        put_rows(later, rows, state)
        state = tail_ref[pl.ds(r, 1), :] * state + get(heads, rows)

    def keep_products(i, n, terms):
        for k in range(0, AT_ONCE, 2):
            place = pl.ds(pl.multiple_of((i * AT_ONCE + k) * CHUNKS, 2 * CHUNKS), 2 * CHUNKS)
            products[place, n * LANES : (n + 1) * LANES] = jnp.concatenate(
                terms[k : k + 2], axis=0
            ).astype(BF16)

    def forward(i, carry):
        steps = [i * AT_ONCE + k for k in range(AT_ONCE)]
        rows = [pl.ds(s, CHUNKS, stride=length) for s in steps]
        a, x, g = stepped((decay, inflow, flow), rows)
        (yg,) = stepped((gx,), rows)
        for k, s in enumerate(steps):
            place = pl.ds(pl.multiple_of(s * CHUNKS, CHUNKS), CHUNKS)
            for index, value in enumerate((a, x, g, yg)):
                for t in range(count):
                    packed[index, t, place, :] = value[k][t]
        for n in range(STATE):
            b = [spread_at(spread, s, n) for s in steps]
            terms = [None] * AT_ONCE
            for t in range(count):
                h = start[t, state_at(n), :]
                for k in range(AT_ONCE):
                    h = a[k][t] * h + x[k][t] * b[k]
                    term = h * g[k][t]
                    terms[k] = term if t == 0 else terms[k] + term
                start[t, state_at(n), :] = h
            keep_products(i, n, terms)
        return carry

    lax.fori_loop(0, length // AT_ONCE, forward, 0)
    mixed[...] += jnp.dot(products[...], pick_c_ref[...], preferred_element_type=F32)
    for t in range(count):
        edge = later[t, state_at(0), :] * start[t, state_at(0), :]
        for n in range(1, STATE):
            edge = edge + later[t, state_at(n), :] * start[t, state_at(n), :]
        log_sum[t] = edge

    def backward(k, carry):
        i = length // AT_ONCE - 1 - k
        steps = [i * AT_ONCE + k for k in range(AT_ONCE)]
        places = [pl.ds(pl.multiple_of(s * CHUNKS, CHUNKS), CHUNKS) for s in steps]
        a, x, g = stepped((packed.at[0], packed.at[1], packed.at[2]), places)
        sums = [[None] * count for _ in steps]
        for n in range(STATE):
            b = [spread_at(spread, s, n) for s in steps]
            c = [spread_at(spread, s, STATE + n) for s in steps]
            terms = [None] * AT_ONCE
            for t in range(count):
                held = later[t, state_at(n), :]
                for k in range(AT_ONCE - 1, -1, -1):
                    adj = held + g[k][t] * c[k]
                    term = adj * b[k]
                    sums[k][t] = term if n == 0 else sums[k][t] + term
                    term = adj * x[k][t]
                    terms[k] = term if t == 0 else terms[k] + term
                    held = a[k][t] * adj
                later[t, state_at(n), :] = held
            keep_products(i, n, terms)
        for t in range(count):
            total = log_sum[t]
            for k in range(AT_ONCE - 1, -1, -1):
                target = pl.ds(steps[k], CHUNKS, stride=length)
                dx = sums[k][t]
                total = total + packed[3, t, places[k], :] - x[k][t] * dx
                total = jnp.where(a[k][t] == 0.0, 0.0, total)
                gx[t, target, :] = dx
                glog[t, target, :] = total
            log_sum[t] = total
        return carry

    lax.fori_loop(0, length // AT_ONCE, backward, 0)
    mixed[...] += jnp.dot(products[...], pick_b_ref[...], preferred_element_type=F32)

    @pl.when(pl.program_id(0) == pl.num_programs(0) - 1)
    def _():
        for j in range(CHUNKS):
            gbc_ref[j * length : (j + 1) * length, :] = mixed[
                pl.ds(j, length, stride=CHUNKS), :
            ].astype(BF16)

    rate = -jnp.exp(par_ref[0:1, :])
    skip = par_ref[2:3, :]
    u = u_ref[...]
    raw = pre_ref[...] + par_ref[1:2, :]
    step = softplus(raw)
    dx = get(gx, slice(None))
    dlog = get(glog, slice(None))
    gpre = (dlog * rate + dx * u) * sigmoid(raw)
    sig = sigmoid(gate)
    gu_ref[...] = (g * skip + dx * step).astype(BF16)
    gz_ref[...] = (
        grad_ref[...] * (scanned_ref[...] + skip * u) * (sig * (1.0 + gate * (1.0 - sig)))
    ).astype(BF16)
    gp_ref[...] = gpre.astype(BF16)
    gpar_ref[0:1, :] = jnp.sum(dlog * step, axis=0, keepdims=True) * rate
    gpar_ref[1:2, :] = jnp.sum(gpre, axis=0, keepdims=True)
    gpar_ref[2:3, :] = jnp.sum(g * u, axis=0, keepdims=True)
    gpar_ref[3:8, :] = jnp.zeros((5, count * LANES), F32)


class ScanCalls:
    def __init__(self, rows, wide, me):
        self.rows, self.wide, self.me = rows, wide, me
        self.length = rows // CHUNKS
        tiles = wide // LANES
        self.count = 2 if tiles % 2 == 0 else 1
        self.lanes = self.count * LANES
        self.steps = tiles // self.count
        self.bc_spec = pl.BlockSpec((rows, LANES), lambda t: (0, 3 * tiles))
        self.keep_spec = pl.BlockSpec((rows, LANES), lambda t: (0, 0))
        self.tile = pltpu.VMEM((self.count, rows, LANES), F32)
        self.thin = pltpu.VMEM((rows, LANES), F32)
        self.spread = pltpu.VMEM((rows, 2 * STATE * LANES), F32)
        self.packed = STATE * CHUNKS
        self.states = pltpu.VMEM((self.count, self.packed, LANES), F32)

    def tall(self, part):
        steps = self.steps
        return pl.BlockSpec((self.rows, self.lanes), lambda t: (0, part * steps + t))

    def flat(self, height):
        return pl.BlockSpec((height, self.lanes), lambda t: (0, t))

    def out(self, height, kind=F32):
        return jax.ShapeDtypeStruct((height, self.wide), kind)

    def call(self, kernel, in_specs, out_specs, out_shape, scratch, flops, moved):
        return pl.pallas_call(
            functools.partial(kernel, self.length, self.count),
            grid=(self.steps,),
            in_specs=[pl.BlockSpec(memory_space=pltpu.SMEM)] + in_specs,
            out_specs=out_specs,
            out_shape=out_shape,
            scratch_shapes=scratch,
            compiler_params=kernel_params(),
            cost_estimate=cost(flops, moved),
        )

    def before(self, proj, keep, par):
        return self.call(
            before_kernel,
            [self.tall(0), self.tall(2), self.bc_spec, self.keep_spec, self.flat(8)],
            [self.flat(self.packed), self.flat(CHUNKS), self.flat(STATE + 8)],
            [self.out(self.packed), self.out(CHUNKS), self.out(STATE + 8)],
            [self.tile, self.tile, self.states],
            2e9,
            self.rows * self.wide * 8,
        )(self.me, proj, proj, proj, keep, par)

    def scan(self, proj, keep, par, ends, tail, carried):
        return self.call(
            scan_kernel,
            [self.tall(0), self.tall(1), self.tall(2), self.bc_spec, self.keep_spec, self.flat(8)]
            + [self.flat(self.packed), self.flat(CHUNKS), self.flat(STATE)],
            [self.tall(0), self.tall(0), self.flat(self.packed)],
            [self.out(self.rows, BF16), self.out(self.rows), self.out(self.packed)],
            [self.spread, self.thin, self.tile, self.tile, self.tile, self.states, self.states],
            8e9,
            self.rows * self.wide * 18,
        )(self.me, proj, proj, proj, proj, keep, par, ends, tail, carried)

    def after(self, grad_mid, proj, keep, par, tail):
        return self.call(
            after_kernel,
            [self.tall(0), self.tall(1), self.tall(2), self.bc_spec, self.keep_spec, self.flat(8)]
            + [self.flat(CHUNKS)],
            [self.flat(self.packed), self.flat(STATE)],
            [self.out(self.packed), self.out(STATE)],
            [self.tile, self.tile, self.states],
            2e9,
            self.rows * self.wide * 12,
        )(self.me, grad_mid, proj, proj, proj, keep, par, tail)

    def back(self, grad_mid, proj, keep, par, tail, scanned, start, heads, carried):
        lane = jnp.arange(STATE * LANES, dtype=jnp.int32)[:, None] // LANES
        column = jnp.arange(LANES, dtype=jnp.int32)[None, :]
        pick_b = (lane == column).astype(BF16)
        pick_c = (lane + STATE == column).astype(BF16)
        pick_spec = pl.BlockSpec((STATE * LANES, LANES), lambda t: (0, 0))
        products = pltpu.VMEM((self.rows, STATE * LANES), BF16)
        return self.call(
            scan_back_kernel,
            [self.tall(0), self.tall(0), self.tall(1), self.tall(2), self.bc_spec]
            + [self.keep_spec, self.flat(8), self.flat(CHUNKS), self.tall(0)]
            + [self.flat(self.packed), self.flat(self.packed), self.flat(STATE)]
            + [pick_spec, pick_spec],
            [self.tall(0), self.tall(0), self.tall(0), self.keep_spec, self.flat(8)],
            [self.out(self.rows, BF16)] * 3
            + [jax.ShapeDtypeStruct((self.rows, LANES), BF16), self.out(8)],
            [self.spread, products] + [self.tile] * 5
            + [pltpu.VMEM((4, self.count, self.rows, LANES), F32)]
            + [self.states] * 3 + [self.thin, pltpu.VMEM((self.count, CHUNKS, LANES), F32)],
            4e10,
            self.rows * self.wide * 30,
        )(self.me, grad_mid, proj, proj, proj, proj, keep, par, tail, scanned, start, heads, carried, pick_b, pick_c)


def allowed_at(base, low_ref):
    shape = (low_ref.shape[0], WINDOW + low_ref.shape[0])
    place = lax.broadcasted_iota(jnp.int32, shape, 1) + base
    own = lax.broadcasted_iota(jnp.int32, shape, 0) + (base + WINDOW)
    return (place >= low_ref[...]) & (place <= own)


def scores_of(allowed, q, keys):
    scores = lax.dot_general(q, keys, (((1,), (1,)), ((), ())), preferred_element_type=F32)
    return jnp.where(allowed, scores, -1e30)


def turn_slots(value):
    return jnp.concatenate(
        [pltpu.roll(value[:, wide_lanes(t)], HEAD, 1) for t in range(2)], axis=1
    )


def lay_out(me_ref, block, parts, kv):
    for k, part in enumerate(parts):
        for j in range(CHUNKS):
            source = pl.multiple_of((me_ref[0] ^ j) * block, block)
            target = slice((k * CHUNKS + j) * block, (k * CHUNKS + j + 1) * block)
            value = part[pl.ds(source, block), :]
            kv[0, target, :] = value
            kv[1, target, :] = turn_slots(value.astype(F32)).astype(BF16)


def half_of(lane, h):
    return (lane < HEAD) if h % 2 == 0 else (lane >= HEAD)


def attend_kernel(heads, hops, me_ref, q_ref, *refs):
    parts, (low_ref, out_ref, log_ref, kv) = refs[: hops + 1], refs[hops + 1 :]
    block = q_ref.shape[0]

    @pl.when(pl.program_id(0) == 0)
    def _():
        lay_out(me_ref, block, parts, kv)

    base = (pl.program_id(0) ^ me_ref[0]) * block + (hops * CHUNKS * block - WINDOW)
    window = pl.ds(pl.multiple_of(base, LANES), WINDOW + block)
    lane = lax.broadcasted_iota(jnp.int32, (block, LANES), 1)
    logs = jnp.zeros((block, LANES), F32)
    allowed = allowed_at(base, low_ref)
    scores = []
    for h in range(heads):
        q = q_ref[:, wide_lanes(h // 2)].astype(F32) * 0.125
        q = jnp.where(half_of(lane, h), q, 0.0).astype(BF16)
        scores.append(scores_of(allowed, q, kv[me_ref[1 + h], window, :LANES]))
    softs, totals = [], []
    for h in range(heads):
        top = jnp.max(scores[h], axis=1, keepdims=True)
        soft = jnp.exp(scores[h] - top)
        total = jnp.sum(soft, axis=1, keepdims=True)
        softs.append(soft.astype(BF16))
        totals.append(1.0 / total)
        logs = jnp.where(lane == h, top + jnp.log(total), logs)
    mixes = []
    for h in range(heads):
        mix = jnp.dot(softs[h], kv[me_ref[1 + h], window, LANES:], preferred_element_type=F32)
        mixes.append(mix * totals[h])
        if h % 2:
            out_ref[:, wide_lanes(h // 2)] = jnp.where(lane < HEAD, mixes[h - 1], mixes[h]).astype(BF16)
    log_ref[...] = logs


def attend_back_kernel(heads, hops, me_ref, q_ref, *refs):
    parts, refs = refs[: hops + 1], refs[hops + 1 :]
    low_ref, log_ref, grad_ref, gq_ref = refs[:4]
    gparts, (kv, gkv) = refs[4 : hops + 5], refs[hops + 5 :]
    block = q_ref.shape[0]

    @pl.when(pl.program_id(0) == 0)
    def _():
        lay_out(me_ref, block, parts, kv)
        gkv[...] = jnp.zeros_like(gkv)

    base = (pl.program_id(0) ^ me_ref[0]) * block + (hops * CHUNKS * block - WINDOW)
    window = pl.ds(pl.multiple_of(base, LANES), WINDOW + block)
    lane = lax.broadcasted_iota(jnp.int32, (block, LANES), 1)
    across = (((0,), (0,)), ((), ()))
    allowed = allowed_at(base, low_ref)
    first = []
    for h in range(heads):
        part = wide_lanes(h // 2)
        turned = me_ref[1 + h]
        mine = half_of(lane, h)
        q = jnp.where(mine, q_ref[:, part].astype(F32) * 0.125, 0.0).astype(BF16)
        grad = jnp.where(mine, grad_ref[:, part].astype(F32), 0.0).astype(BF16)
        scores = scores_of(allowed, q, kv[turned, window, :LANES])
        gsoft = lax.dot_general(
            grad, kv[turned, window, LANES:], (((1,), (1,)), ((), ())), preferred_element_type=F32
        )
        first.append((q, grad, scores, gsoft))
    second = []
    for h in range(heads):
        q, grad, scores, gsoft = first[h]
        soft = jnp.exp(scores - log_ref[:, h : h + 1])
        delta = jnp.sum(soft * gsoft, axis=1, keepdims=True)
        second.append((soft.astype(BF16), (soft * (gsoft - delta)).astype(BF16)))
    gqs = []
    for h in range(heads):
        part = wide_lanes(h // 2)
        turned = me_ref[1 + h]
        q, grad = first[h][:2]
        soft, gscore = second[h]
        gqs.append(
            jnp.dot(gscore, kv[turned, window, :LANES], preferred_element_type=F32) * 0.125
        )
        gkv[turned, window, :LANES] += lax.dot_general(
            gscore, q, across, preferred_element_type=F32
        )
        gkv[turned, window, LANES:] += lax.dot_general(
            soft, grad, across, preferred_element_type=F32
        )
        if h % 2:
            gq_ref[:, part] = jnp.where(lane < HEAD, gqs[h - 1], gqs[h]).astype(BF16)

    @pl.when(pl.program_id(0) == pl.num_programs(0) - 1)
    def _():
        for k, part in enumerate(gparts):
            for j in range(CHUNKS):
                target = pl.multiple_of((me_ref[0] ^ j) * block, block)
                source = slice((k * CHUNKS + j) * block, (k * CHUNKS + j + 1) * block)
                part[pl.ds(target, block), :] = (
                    gkv[0, source, :] + turn_slots(gkv[1, source, :])
                ).astype(part.dtype)


def attend_specs(rows, hops):
    block = rows // CHUNKS
    by_row = lambda width: pl.BlockSpec((block, width), lambda b: (b, 0))
    whole = [pl.BlockSpec((rows, 2 * LANES), lambda b: (0, 0))] * (hops + 1)
    total = (hops + 1) * rows
    return by_row, whole, total, pl.BlockSpec(memory_space=pltpu.SMEM)


def attend(heads, me, q, kvs, low):
    rows, wide = q.shape
    by_row, whole, total, scalar = attend_specs(rows, len(kvs) - 1)
    return pl.pallas_call(
        functools.partial(attend_kernel, heads, len(kvs) - 1),
        grid=(CHUNKS,),
        in_specs=[scalar, by_row(wide), *whole, by_row(1)],
        out_specs=[by_row(wide), by_row(LANES)],
        out_shape=[
            jax.ShapeDtypeStruct((rows, wide), BF16),
            jax.ShapeDtypeStruct((rows, LANES), F32),
        ],
        scratch_shapes=[pltpu.VMEM((2, total, 2 * LANES), BF16)],
        compiler_params=kernel_params(),
        cost_estimate=cost(6e9, 8e6),
    )(me, q, *kvs, low)


def attend_back(heads, me, q, kvs, low, logs, grad):
    rows, wide = q.shape
    by_row, whole, total, scalar = attend_specs(rows, len(kvs) - 1)
    part = jax.ShapeDtypeStruct((rows, 2 * LANES), BF16)
    own = jax.ShapeDtypeStruct((rows, 2 * LANES), F32)
    return pl.pallas_call(
        functools.partial(attend_back_kernel, heads, len(kvs) - 1),
        grid=(CHUNKS,),
        in_specs=[scalar, by_row(wide), *whole, by_row(1), by_row(LANES), by_row(wide)],
        out_specs=[by_row(wide), *whole],
        out_shape=[jax.ShapeDtypeStruct((rows, wide), BF16)] + [part] * (len(kvs) - 1) + [own],
        scratch_shapes=[
            pltpu.VMEM((2, total, 2 * LANES), BF16),
            pltpu.VMEM((2, total, 2 * LANES), F32),
        ],
        compiler_params=kernel_params(),
        cost_estimate=cost(3e10, 1.2e7),
    )(me, q, *kvs, low, logs, grad)


def swap_cores(value):
    return lax.ppermute(value, "core", [(0, 1), (1, 0)])


def from_peer(value, k):
    return lax.ppermute(value, "tp", [(n, n ^ k) for n in range(lax.axis_size("tp"))])


def team_gather(rows):
    tps = lax.axis_size("tp")
    got = {k: from_peer(rows, k) for k in range(tps - 1, 0, -1)}
    own = jnp.concatenate([rows] + [got[k] for k in range(1, tps)], axis=0)
    return jnp.concatenate([own, swap_cores(own)], axis=0)


def team_pair(values):
    half = values.shape[0] // CORES
    block = half // lax.axis_size("tp")
    other = swap_cores(values[half:])
    low = (values[:half].astype(F32) + other.astype(F32)).astype(BF16)
    return low, values[:block].astype(F32) + other[:block].astype(F32)


def peers_sum(low, total):
    tps = lax.axis_size("tp")
    block = low.shape[0] // tps
    for part in [from_peer(low[k * block : (k + 1) * block], k) for k in range(tps - 1, 0, -1)]:
        total = total + part.astype(F32)
    return total


def team_scatter(values):
    low, total = team_pair(values)
    return peers_sum(low, total), low


def peer_reduce(value):
    tps, own = lax.axis_size("tp"), lax.axis_index("tp")
    block = round_up(value.shape[1], tps * LANES) // tps
    value = jnp.pad(value, ((0, 0), (0, tps * block - value.shape[1])))
    parts = [lax.dynamic_slice_in_dim(value, (own ^ k) * block, block, 1) for k in range(tps)]
    total = parts[0]
    for k in range(1, tps):
        total = total + from_peer(parts[k].astype(BF16), k).astype(F32)
    return total.astype(BF16)


def peer_spread(part):
    tps, own = lax.axis_size("tp"), lax.axis_index("tp")
    block = part.shape[1]
    whole = jnp.zeros((part.shape[0], tps * block), BF16)
    for k in range(tps):
        got = from_peer(part, k) if k else part
        whole = lax.dynamic_update_slice_in_dim(whole, got, (own ^ k) * block, 1)
    return whole


def shifted(value, steps):
    count = lax.axis_size("chip")
    leading, last = (max(0, -steps), min(count, count - steps))
    return lax.ppermute(value, "chip", [(k, k + steps) for k in range(leading, last)])


def behind(value, *others):
    if len(others) > 1:
        value = behind(value, *others[:-1])
    other = others[-1]
    last = other[(slice(-1, None),) * other.ndim].reshape((1,) * value.ndim)
    return value + (last * 0).astype(value.dtype)


def chip_gather(value):
    chips = lax.axis_size("chip")
    if chips != 4:
        return lax.all_gather(value, "chip")
    own = lax.axis_index("chip")
    got = jnp.stack(
        [value] + [lax.ppermute(value, "chip", [(n, n ^ k) for n in range(chips)]) for k in range(1, chips)]
    )
    return jnp.concatenate([lax.dynamic_slice_in_dim(got, own ^ k, 1, 0) for k in range(chips)])


def by_core(mine, other):
    first = lax.axis_index("core") == 0
    return jnp.where(first, mine, other), jnp.where(first, other, mine)


def to_rows(values):
    tps = lax.axis_size("tp")
    half = values.shape[0] // CORES
    block = half // tps
    wide = CORES * values.shape[1]
    pair = jnp.concatenate(by_core(values[:half], swap_cores(values[half:])), axis=1)
    got = [pair[:block]] + [from_peer(pair[k * block : (k + 1) * block], k) for k in range(1, tps)]
    whole = jnp.zeros((block, tps * wide), values.dtype)
    for k in range(tps):
        place = (lax.axis_index("tp") ^ k) * wide
        whole = lax.dynamic_update_slice_in_dim(whole, got[k], place, 1)
    return whole


def to_columns(values):
    tps = lax.axis_size("tp")
    wide = values.shape[1] // tps
    parts = [
        lax.dynamic_slice_in_dim(values, (lax.axis_index("tp") ^ k) * wide, wide, 1)
        for k in range(tps)
    ]
    pair = jnp.concatenate([parts[0]] + [from_peer(parts[k], k) for k in range(1, tps)], axis=0)
    mine, other = by_core(pair[:, : wide // CORES], pair[:, wide // CORES :])
    return jnp.concatenate([mine, swap_cores(other)], axis=0)


def core_pair(shard, rows):
    core = lax.axis_index("core")
    mine = lax.dynamic_index_in_dim(shard, core, 1, False)
    other = swap_cores(lax.dynamic_index_in_dim(shard, 1 - core, 1, False))
    pair = jnp.concatenate(by_core(mine, other), axis=0)
    return jnp.pad(pair, ((0, rows - pair.shape[0]), (0, 0)))


def summed_rows(full):
    return behind(lax.psum_scatter(full, "chip", scatter_dimension=0, tiled=True), full)


def split_cores(rows, count):
    rows = rows[: CORES * count].reshape(CORES, count, -1)
    core = lax.axis_index("core")
    mine = lax.dynamic_index_in_dim(rows, core, 0, False)
    return mine, swap_cores(lax.dynamic_index_in_dim(rows, 1 - core, 0, False))


def share_columns(pair):
    tps = lax.axis_size("tp")
    whole = jnp.concatenate([pair] + [from_peer(pair, k) for k in range(1, tps)], axis=0)
    own = lax.axis_index("tp") * CORES + lax.axis_index("core")
    return jnp.concatenate(
        [lax.dynamic_slice_in_dim(whole, own ^ k, 1, 0) for k in range(CORES * tps)], axis=0
    )


def body(
    x_in, lengths, w_q, w_kv, w_o, input_weight, a_log, dt_bias, d_skip,
    w_bc, w_out, gains, gate_up_weight, w_down, cotangent,
):
    chips, tps = lax.axis_size("chip"), lax.axis_size("tp")
    chip, core, tp = (lax.axis_index(name) for name in ("chip", "core", "tp"))
    team = CORES * tps
    unit = tp * CORES + core
    layers, shard_rows, width = w_q.shape
    rows_own, features = x_in.shape
    part = features // chips
    part_wide = round_up(features, LANES) // chips
    padded = part_wide * chips
    rows = rows_own * team
    hops = -(-WINDOW // rows)
    kv_half = w_kv.shape[2] // 2
    heads_here = -(-HEADS // team)
    q_wide = heads_here * HEAD
    slot_wide = SLOTS * HEAD
    channels = a_log.shape[1] // CORES
    wide = round_up(channels, LANES)
    hidden_here = gate_up_weight.shape[3] // CORES
    hidden_wide = round_up(hidden_here, LANES)
    me = (core * tps + tp).astype(jnp.int32)
    me_array = jnp.reshape(me, (1,))
    scan = ScanCalls(rows, wide, me_array)
    sums = [None] * layers

    order = jnp.arange(team, dtype=jnp.int32) ^ me
    local = order[:, None] * rows_own + jnp.arange(rows_own, dtype=jnp.int32)[None, :]
    places = chip * rows + local.reshape(rows)
    starts = (jnp.cumsum(lengths) - lengths).astype(jnp.int32)
    reached = places[:, None] >= starts[None, :]
    opening = jnp.any(places[:, None] == starts[None, :], axis=1)
    keep = jnp.broadcast_to((1.0 - opening.astype(F32))[:, None], (rows, LANES))
    first = jnp.max(jnp.where(reached, starts[None, :], 0), axis=1)
    low = jnp.maximum(first, places - (WINDOW - 1)) - (chip - hops) * rows
    low = low[:, None]

    head_ids = unit * heads_here + jnp.arange(heads_here, dtype=jnp.int32)
    slot_ids = head_ids // GROUP - (unit * heads_here) // GROUP
    turns = (slot_ids ^ jnp.arange(heads_here, dtype=jnp.int32)) & 1
    attend_array = jnp.concatenate([me_array, turns.astype(jnp.int32)])

    def spaced(values):
        values = values.reshape(values.shape[:-1] + (chips, part))
        return pad_lanes(values, part_wide).reshape(values.shape[:-2] + (padded,))

    def unspaced(values):
        values = values.reshape(values.shape[:-1] + (chips, part_wide))[..., :part]
        return values.reshape(values.shape[:-2] + (features,))

    def pad_lanes(values, size):
        return jnp.pad(values, [(0, 0)] * (values.ndim - 1) + [(0, size - values.shape[-1])])

    def kv_columns(layer, index):
        base = (index * heads_here) // GROUP * HEAD
        whole = jnp.pad(w_kv[layer].reshape(shard_rows, 2, kv_half), ((0, 0), (0, 0), (0, slot_wide)))
        return lax.dynamic_slice_in_dim(whole, base, slot_wide, 2).reshape(shard_rows, 2 * slot_wide)

    place = chip * CORES + core

    def prepare_mixer_in(layer):
        ins = input_weight[layer].reshape(shard_rows, 3, CORES, channels)
        ins = pad_lanes(ins.transpose(0, 2, 1, 3), wide).reshape(shard_rows, CORES, 3 * wide)
        bcs = lax.dynamic_slice_in_dim(w_bc[layer], place * shard_rows, shard_rows, 0)
        bcs = jnp.broadcast_to(pad_lanes(bcs, LANES)[:, None], (shard_rows, CORES, LANES))
        qs = lax.dynamic_slice_in_dim(
            pad_lanes(w_q[layer], team * q_wide), tp * CORES * q_wide, CORES * q_wide, 1
        ).reshape(shard_rows, CORES, q_wide)
        kvs = jnp.stack([kv_columns(layer, tp * CORES + k) for k in range(CORES)], axis=1)
        return core_pair(jnp.concatenate([ins, bcs, qs, kvs], axis=2), part_wide)

    def prepare_mixer_out(layer):
        return core_pair(
            pad_lanes(w_out[layer].T.reshape(shard_rows, CORES, channels), wide), part_wide
        )

    def prepare_ffn(layer):
        gus = gate_up_weight[layer].reshape(shard_rows, 2, CORES, hidden_here)
        gus = pad_lanes(gus.transpose(0, 2, 1, 3), hidden_wide)
        gus = gus.reshape(shard_rows, CORES, 2 * hidden_wide)
        downs = pad_lanes(w_down[layer].T.reshape(shard_rows, CORES, hidden_here), hidden_wide)
        return core_pair(jnp.concatenate([gus, downs], axis=2), part_wide)

    def of_chips(pair):
        return lax.all_gather(pair, "chip", axis=0, tiled=True)

    def scan_params(layer):
        mine = [
            lax.dynamic_slice_in_dim(part[layer], core * channels, channels, 0)
            for part in (a_log, dt_bias, d_skip)
        ]
        return jnp.pad(jnp.stack(mine), ((0, 5), (0, wide - channels)))

    def chain(everything, back):
        state = jnp.zeros(everything[0][0].shape, F32)
        order = range(chips - 1, -1, -1) if back else range(chips)
        for k in order:
            counts = (k > chip) if back else (k < chip)
            new = everything[1][k][None, :] * state + everything[0][k]
            state = jnp.where(counts, new, state)
        return state

    norm = functools.partial(rms_scale, features)
    mix = functools.partial(branch_mix, features)

    def norm_in(stream, layer):
        return team_gather(norm(stream, gains[layer, 0]).astype(BF16))

    def forward_layer(stream, normed_all, layer, weights, aside=None):
        w_in, w_ssm, w_attn, w_mamba, w_attn_out, w_gu, w_dn = weights
        gain = gains[layer]
        par = scan_params(layer)
        qkv = dot(normed_all, w_attn, BF16)
        kv = qkv[:, q_wide:]
        others = [team_gather(behind(aside, kv))] if aside is not None else []
        kvs = [shifted(kv, hop) for hop in range(hops, 0, -1)] + [kv]
        proj = behind(dot(normed_all, w_ssm), kv)
        ends, tail, dev = scan.before(proj, keep, par)
        devs = chip_gather(behind(dev, kvs[0]))
        chip_decay = devs[:, STATE]
        carried = chain((devs[:, :STATE], chip_decay), False)
        q = qkv[:, :q_wide]
        attended, logs = attend(heads_here, attend_array, q, kvs, behind(low, dev))
        own_attended = to_rows(attended)[:, :width]
        mid, scanned, start = scan.scan(
            proj, keep, behind(par, attended, *others), ends, tail, carried
        )
        mamba_out, low_out = team_scatter(dot_nt(behind(mid, own_attended), w_mamba, BF16))
        attn_out = dot(behind(own_attended, low_out), w_attn_out)
        middle = stream + mix(attn_out, mamba_out, gain[1], gain[2])
        ffn_all = team_gather(norm(middle, gain[3]).astype(BF16))
        gate_up = dot(ffn_all, w_gu)
        hidden = swiglu(gate_up).astype(BF16)
        ffn_part = dot_nt(hidden, w_dn, BF16)
        kept = dict(
            stream=stream, normed_all=normed_all, q=q, kvs=kvs, logs=logs,
            own_attended=own_attended, proj=proj, tail=tail, chip_decay=chip_decay, mid=mid,
            scanned=scanned, start=start, attn_out=attn_out, mamba_out=mamba_out, middle=middle,
            ffn_all=ffn_all, gate_up=gate_up, hidden=hidden, par=par,
        )
        return middle, ffn_part, kept, others

    def backward_layer(grad_out, grad_all, layer, weights, kept, aside):
        early = layer == 0
        w_in, w_ssm, w_attn, w_mamba, w_attn_out, w_gu, w_dn = weights
        gain = gains[layer]
        normed_all = kept["normed_all"]
        grad_hidden = dot(grad_all, w_dn)
        _, swiglu_pull = jax.vjp(swiglu, kept["gate_up"])
        grad_gu = swiglu_pull(grad_hidden)[0].astype(BF16)
        partial = dot_nt(grad_gu, w_gu, BF16)
        grad_ffn, low_ffn = team_scatter(partial)
        full_ffn = jnp.concatenate(
            [
                dot_tn(kept["ffn_all"], behind(grad_gu, low_ffn), BF16),
                dot_tn(grad_all, behind(kept["hidden"], low_ffn), BF16),
            ],
            axis=1,
        )
        ffn_sums = summed_rows(full_ffn)
        grad_ffn = behind(grad_ffn, full_ffn)
        _, norm_pull = jax.vjp(norm, kept["middle"], gain[3])
        grad_mid_norm, grad_gain_ffn = norm_pull(grad_ffn)
        grad_middle = grad_out + grad_mid_norm
        _, mix_pull = jax.vjp(mix, kept["attn_out"], kept["mamba_out"], gain[1], gain[2])
        grad_attn, grad_mamba, grad_gain_attn, grad_gain_mamba = mix_pull(grad_middle)
        grad_mamba_all = team_gather(grad_mamba.astype(BF16))
        grad_attn = grad_attn.astype(BF16)
        grad_att = pad_lanes(dot_nt(grad_attn, w_attn_out, BF16), team * q_wide)
        grad_att = to_columns(grad_att)
        full_o = dot_tn(spaced(kept["own_attended"]), behind(grad_attn, grad_att), BF16)
        gq, *gkvs = attend_back(
            heads_here, attend_array, kept["q"], kept["kvs"], low, kept["logs"], grad_att
        )
        gkv = gkvs[hops]
        for hop in range(1, hops + 1):
            gkv = gkv + shifted(gkvs[hops - hop], -hop).astype(F32)
        grad_qkv = jnp.concatenate([gq, gkv.astype(BF16)], axis=1)
        grad_mid = dot(grad_mamba_all, w_mamba)
        par = kept["par"]
        heads, dev = scan.after(grad_mid, kept["proj"], keep, behind(par, gq), kept["tail"])
        devs = chip_gather(dev)
        carried = chain((devs, kept["chip_decay"]), True)
        full_out = dot_tn(grad_mamba_all, behind(kept["mid"], dev), BF16)
        if early:
            full_qkv = dot_tn(normed_all, behind(grad_qkv, dev), BF16)
            full_mix = jnp.concatenate([full_qkv, full_out, full_o], axis=1)
            mix_sums = summed_rows(full_mix)
            par = behind(par, full_mix)
        else:
            par = behind(par, full_out, full_o, ffn_sums)
        gates, sides = aside()
        par = behind(par, *gates)
        gu, gz, gp, gbc, gpar = scan.back(
            grad_mid, kept["proj"], keep, par, kept["tail"], kept["scanned"], kept["start"], heads, carried
        )
        gbc = behind(gbc, *sides)
        grad_proj = jnp.concatenate([gu, gz, gp, gbc, grad_qkv], axis=1)
        if early:
            full_in = dot_tn(normed_all, grad_proj[:, : 3 * wide + LANES], BF16)
            ssm_sums = summed_rows(full_in)
            partial = dot_nt(behind(grad_proj, full_in), w_in, BF16)
            grad_normed, low_normed = team_scatter(partial)
        else:
            partial = dot_nt(grad_proj, w_in, BF16)
            grad_normed, low_normed = team_scatter(partial)
            full_in = dot_tn(normed_all, behind(grad_proj, low_normed), BF16)
            grad_normed = behind(grad_normed, full_in)
            mix_sums = summed_rows(jnp.concatenate([full_in, full_out, full_o], axis=1))
            ssm_sums = mix_sums[:, : 3 * wide + LANES]
            mix_sums = mix_sums[:, 3 * wide + LANES :]
        _, in_pull = jax.vjp(norm, kept["stream"], gain[0])
        grad_stream_norm, grad_gain_in = in_pull(grad_normed)
        grad_gains = jnp.stack([grad_gain_in, grad_gain_attn, grad_gain_mamba, grad_gain_ffn])
        small = jnp.concatenate([grad_gains.reshape(-1), gpar[:3, :channels].reshape(-1)])
        later = dict(ffn=ffn_sums, ssm=ssm_sums, mix=mix_sums, small=small)
        return grad_middle + grad_stream_norm, later

    gains = spaced(gains)
    stream = spaced(x_in).astype(F32)
    cotangent = spaced(cotangent)
    normed_all = norm_in(stream, 0)
    pairs = [(prepare_mixer_in(l), prepare_mixer_out(l), prepare_ffn(l)) for l in range(layers)]
    weights = []
    for layer in range(layers):
        ins, outs, ffn = pairs[layer]
        if layer == 0:
            ins = of_chips(ins)
            lead = normed_all
        else:
            ins = of_chips(behind(ins, lead))
        outs = of_chips(behind(outs, lead))
        o = lax.all_gather(behind(spaced(w_o[layer]), lead), ("chip", "core"), axis=0, tiled=True)
        ffn = of_chips(behind(ffn, lead))
        first = 3 * wide + LANES
        weights.append(
            (
                ins, ins[:, :first], ins[:, first:], outs, o,
                ffn[:, : 2 * hidden_wide], ffn[:, 2 * hidden_wide :],
            )
        )
    kept = []
    for layer in range(layers):
        if layer:
            normed_all = norm_in(stream, layer)
        middle, ffn_part, saved, others = forward_layer(
            stream, normed_all, layer, weights[layer], None if layer else cotangent
        )
        if layer == 0:
            grad_all = others[0]
        kept.append(saved)
        if layer + 1 < layers:
            stream = middle + team_scatter(ffn_part)[0]
    grad_stream = cotangent.astype(F32)
    shares = [None] * layers
    grad_os = [None] * layers
    out_sums = [None] * layers

    qkv_wide = q_wide + 2 * slot_wide

    def mix_parts(layer):
        mine, other = split_cores(sums[layer]["mix"], shard_rows)
        ours = mine[:, qkv_wide + wide :].astype(F32) + other[:, qkv_wide + wide :].astype(F32)
        out_sums[layer] = (mine[:, qkv_wide : qkv_wide + wide], other[:, qkv_wide : qkv_wide + wide])
        return jnp.stack([mine[:, :qkv_wide], other[:, :qkv_wide]]), ours

    for layer in range(layers - 1, -1, -1):
        if layer + 1 < layers:
            grad_all = team_gather(grad_stream.astype(BF16))
        found = []

        def aside(layer=layer, found=found):
            if layer + 1 == layers:
                low_out, total = team_pair(ffn_part)
                found.append(peers_sum(low_out, total))
                return (low_out,), found
            pair, ours = mix_parts(layer + 1)
            shares[layer + 1] = share_columns(pair)
            grad_os[layer + 1] = peer_spread(peer_reduce(ours))
            return (pair, ours), (shares[layer + 1], grad_os[layer + 1])

        grad_stream, sums[layer] = backward_layer(
            grad_stream, grad_all, layer, weights[layer], kept[layer], aside
        )
        if layer + 1 == layers:
            block_out = unspaced((middle + found[0]).astype(BF16))
    pair, ours = mix_parts(0)
    grad_os[0] = peer_spread(peer_reduce(ours))
    shares[0] = share_columns(pair)

    shared = jnp.stack(shares).transpose(0, 2, 1, 3)
    grad_o = unspaced(jnp.stack(grad_os)[..., :padded]).astype(F32)
    grad_q = shared[..., :q_wide].reshape(layers, shard_rows, team * q_wide)
    grad_q = grad_q[..., :width].astype(F32)
    kv_parts = shared[..., q_wide:].astype(F32)
    kv_parts = kv_parts.reshape(layers, shard_rows, team, 2, SLOTS, HEAD)
    kv_heads = []
    for head in range(KV_HEADS):
        terms = [
            kv_parts[:, :, k, :, slot]
            for k in range(team)
            for slot in range(SLOTS)
            if (k * heads_here) // GROUP + slot == head
        ]
        kv_heads.append(sum(terms[1:], terms[0]))
    grad_kv = jnp.stack(kv_heads, axis=3).reshape(layers, shard_rows, 2 * kv_half)
    ssm_sums = [split_cores(parts["ssm"], shard_rows) for parts in sums]
    ffn_sums = [split_cores(parts["ffn"], shard_rows) for parts in sums]

    def halves(sums_of, begin, end):
        return [
            jnp.stack(by_core(*(part[:, begin:end] for part in parts))).astype(F32)
            for parts in sums_of
        ]

    grad_in = jnp.stack(
        [
            pair.reshape(CORES, shard_rows, 3, wide)[..., :channels]
            .transpose(1, 2, 0, 3)
            .reshape(shard_rows, 3, CORES * channels)
            for pair in halves(ssm_sums, 0, 3 * wide)
        ]
    )
    grad_out = jnp.stack(
        [
            pair.transpose(0, 2, 1).reshape(CORES * channels, shard_rows)
            for pair in halves(out_sums, 0, channels)
        ]
    )
    grad_gu = jnp.stack(
        [
            pair.reshape(CORES, shard_rows, 2, hidden_wide)[..., :hidden_here]
            .transpose(1, 2, 0, 3)
            .reshape(shard_rows, 2, CORES * hidden_here)
            for pair in halves(ffn_sums, 0, 2 * hidden_wide)
        ]
    )
    grad_down = jnp.stack(
        [
            pair.transpose(0, 2, 1).reshape(CORES * hidden_here, shard_rows)
            for pair in halves(ffn_sums, 2 * hidden_wide, 2 * hidden_wide + hidden_here)
        ]
    )
    small = jnp.sum(chip_gather(jnp.stack([parts["small"] for parts in sums])), axis=0)
    other = swap_cores(small)
    gain_part = small[:, : 4 * padded] + other[:, : 4 * padded]
    ssm_pair = jnp.concatenate(by_core(small[:, 4 * padded :], other[:, 4 * padded :]), axis=1)
    tiny = jnp.concatenate([gain_part, ssm_pair], axis=1)
    bc_part = jnp.concatenate(
        [mine[:, 3 * wide :].astype(F32) + theirs[:, 3 * wide :].astype(F32) for mine, theirs in ssm_sums]
    )
    tiny_got = [from_peer(tiny, k) for k in range(1, tps)]
    bc_got = [from_peer(bc_part.astype(BF16), k) for k in range(1, tps)]
    grad_bc = sum((got.astype(F32) for got in bc_got), bc_part)[:, : 2 * STATE]
    grad_bc = grad_bc.reshape(layers, shard_rows, 2 * STATE)
    gain_full = sum((got[:, : 4 * padded] for got in tiny_got), gain_part)
    gain_full = unspaced(gain_full.reshape(layers, 4, padded))
    ssm_all = jnp.stack([ssm_pair] + [got[:, 4 * padded :] for got in tiny_got])
    ssm_all = jnp.concatenate(
        [lax.dynamic_slice_in_dim(ssm_all, tp ^ k, 1, 0) for k in range(tps)]
    )
    ssm_full = ssm_all.reshape(tps, layers, CORES, 3, channels)
    ssm_full = ssm_full.transpose(1, 3, 0, 2, 4).reshape(layers, 3, team * channels)
    share = team * channels // (chips * CORES)
    ssm_own = lax.dynamic_slice_in_dim(ssm_full, place * share, share, 2)
    grad_gains = lax.dynamic_slice_in_dim(gain_full, place * shard_rows, shard_rows, 2)
    return (
        block_out, unspaced(grad_stream), grad_q, grad_kv, grad_o, grad_in,
        ssm_own[:, 0], ssm_own[:, 1], ssm_own[:, 2], grad_bc, grad_out, grad_gains, grad_gu, grad_down,
    )


def solution(mesh):
    fsdp, tp = mesh.shape["fsdp"], mesh.shape["tp"]
    inner = Mesh(mesh.devices.reshape(fsdp // CORES, CORES, tp), ("chip", "core", "tp"))
    shards = ("chip", "core")
    tokens = P(("chip", "core", "tp"), None)
    by_row = P(None, shards, None)
    return jax.shard_map(
        body,
        mesh=inner,
        in_specs=(
            tokens, P(), by_row, by_row, by_row, P(None, shards, None, "tp"),
            P(None, "tp"), P(None, "tp"), P(None, "tp"), P(), P(None, "tp", shards), P(),
            P(None, shards, None, "tp"), P(None, "tp", shards), tokens,
        ),
        out_specs=(
            tokens, tokens, by_row, by_row, by_row, P(None, shards, None, "tp"),
            P(None, shards), P(None, shards), P(None, shards), by_row, P(None, "tp", shards),
            P(None, None, shards), P(None, shards, None, "tp"), P(None, "tp", shards),
        ),
        check_vma=False,
    )
```
